32 devices in a mesh: page: 16 (over z, y, x), head: 2 (over core).
Axes of the slice: x: 2, y: 2, z: 4, core: 2. Of those that a mesh axis runs over, the one named last changes fastest.
Arguments:
- query: bfloat16 [16, 8192], P('page', 'head'), may hold values from -68 to 68
- key_codes: bfloat16 [128, 8, 1024, 128], P('page', 'head'), may hold values from -6 to 6
- value_codes: bfloat16 [128, 8, 1024, 128], P('page', 'head'), may hold values from -6 to 6
- key_scale: float32 [128, 8, 8], P('page', 'head'), may hold values from 0.5 to 2
- value_scale: float32 [128, 8, 8], P('page', 'head'), may hold values from 0.5 to 8
- out_weight: bfloat16 [8192, 8192], P('head', 'page'), may hold values from -0.0625 to 0.0625
- range_counts: int32 [16], replicated, may hold values from 1 to 16, 128 in all
- last_fill: int32 [16], replicated, may hold values from 1 to 1024
- slot_table: int32 [128], replicated, may hold values from 0 to 127, each once
Outputs:
- mixed: bfloat16 [16, 8192], P('head', 'page')
The draws below stay inside these ranges and needn't reach their ends.
All inputs are finite; a program needn't handle non-finite values.
Results may differ from the reference program's by a relative error of at most 0.0056.
Values may be sent and summed in bfloat16 or wider, within the bound.
No kernel may reach another device: no remote copies, remote signals or barrier semaphores. Data moves between devices by JAX's collectives and lax.ppermute only.
A program may use at most 64 MiB of HBM per device.

```python
import math
import jax
import jax.numpy as jnp
import numpy as np
from jax import lax

D = 8192
QH = 64
KVH = 8
HD = 128
PAGE_TOKENS = 128
RANGE_PAGES = 8
RANGES = 16
GROUP = 8
RANGE_TOK = 1024
ROWS = 16
TOTAL_SLOTS = 128


def draw_query(key, part):
    key = jax.random.fold_in(key, 11)
    base_key = jax.random.fold_in(key, 0)
    value_rows = jnp.clip(jax.random.normal(base_key, (ROWS, QH, HD), jnp.float32), -6.0, 6.0) * 2.5
    return value_rows.reshape(ROWS, QH * HD).astype(jnp.bfloat16)


def with_ends(drawn, key, least, high):
    extent = drawn.shape
    index_at = [jax.random.randint(jax.random.fold_in(key, axis), (), 0, extent[axis]) for axis in range(len(extent))]
    drawn = drawn.at[tuple(index_at)].set(least)
    longest = extent.index(max(extent))
    index_at[longest] = (index_at[longest] + 1) % extent[longest]
    return drawn.at[tuple(index_at)].set(high)


def shard_levels(own_key, extent, cuts, least, largest):
    def one(position, blocks):
        heights = jax.random.uniform(jax.random.fold_in(jax.random.fold_in(own_key, 6), position), (blocks,), jnp.float32, least / len(cuts), largest / len(cuts))
        return jnp.repeat(jnp.exp(heights), extent[position] // blocks).reshape((-1,) + (1,) * (len(extent) - position - 1))

    level = one(*cuts[0])
    for cut in cuts[1:]:
        level = level * one(*cut)
    return level


def profile(number_of, total, most, slope):
    portions = [(1 << 20) // math.isqrt(standing ** slope) + 1 for standing in range(2, number_of + 1)]
    surplus, holding = total - most - (number_of - 1), [1] * (number_of - 1)
    while surplus > 0:
        movable = [i for i in range(number_of - 1) if holding[i] < most]
        mass, left = sum([portions[i] for i in movable]), surplus
        for i in movable:
            addition = min(most - holding[i], max(1, left * portions[i] // mass), surplus)
            holding[i] = holding[i] + addition
            surplus = surplus - addition
    return np.array([most] + holding)


def uneven(own_key, amount, total, bound, skew):
    if amount == 2:
        one = jax.random.randint(own_key, (), max(1, total - bound), min(bound, total - 1) + 1)
        return jnp.stack([one, total - one])
    sizes = jnp.asarray(profile(amount, total, bound, skew), jnp.int32)
    twos = (amount - 1) // 2
    source_of, taker = sizes[1:1 + 2 * twos:2], sizes[2:2 + 2 * twos:2]
    slack = jnp.minimum(source_of - 1, bound - taker)
    passed = jax.random.randint(jax.random.fold_in(own_key, 1), (twos,), 0, 1 << 20) % (slack + 1)
    sizes = sizes.at[1:1 + 2 * twos:2].set(source_of - passed).at[2:2 + 2 * twos:2].set(taker + passed)
    return sizes[jax.random.permutation(jax.random.fold_in(own_key, 2), amount)]


def bell_draw(key, shape, deviation, reach, cuts=(), kind=jnp.bfloat16):
    drawn = jax.random.normal(key, shape, jnp.float32) * deviation
    if len(cuts) > 0:
        drawn = shard_levels(key, shape, cuts, -0.22, 0.18) * drawn
    return jnp.clip(drawn, min=-reach, max=reach).astype(kind)


def setup_inputs(seed: int = 0) -> dict:
    seeds = jax.random.split(jax.random.key(seed), 10)
    return {
        "query": draw_query(jax.random.fold_in(seeds[9], 71), 0),
        "key_codes": bell_draw(seeds[1], (TOTAL_SLOTS, KVH, RANGE_TOK, HD), 1.0, 6.0, ((0, 16), (1, 2))),
        "value_codes": bell_draw(seeds[2], (TOTAL_SLOTS, KVH, RANGE_TOK, HD), 1.0, 6.0, ((0, 16), (1, 2))),
        "key_scale": jnp.clip(jnp.exp(math.log(2.0) - 1.3862944 * jax.random.uniform(seeds[3], (TOTAL_SLOTS, KVH, RANGE_PAGES), jnp.float32) ** shard_levels(seeds[3], (TOTAL_SLOTS, KVH, RANGE_PAGES), ((0, 16), (1, 2)), -0.2, 0.2)), 0.5, 2.0),
        "value_scale": jnp.clip(jnp.exp(math.log(8.0) - 2.7725887 * jax.random.uniform(seeds[4], (TOTAL_SLOTS, KVH, RANGE_PAGES), jnp.float32) ** shard_levels(seeds[4], (TOTAL_SLOTS, KVH, RANGE_PAGES), ((0, 16), (1, 2)), -0.2, 0.2)), 0.5, 8.0),
        "out_weight": bell_draw(seeds[5], (QH * HD, D), (QH * HD) ** -0.5, 0.0625, ((0, 2), (1, 16))),
        "range_counts": uneven(seeds[6], ROWS, TOTAL_SLOTS, RANGES, 2).astype(jnp.int32),
        "last_fill": with_ends(jax.random.randint(seeds[7], (ROWS,), 1, RANGE_TOK + 1), jax.random.fold_in(seeds[7], 1), 1, RANGE_TOK).astype(jnp.int32),
        "slot_table": jax.random.permutation(seeds[8], TOTAL_SLOTS).astype(jnp.int32),
    }


def reference(query, key_codes, value_codes, key_scale, value_scale, out_weight, range_counts, last_fill, slot_table):
    inclusive = jnp.cumsum(range_counts).astype(jnp.int32)
    exclusive = (inclusive - range_counts).astype(jnp.int32)
    lengths = ((range_counts - 1) * RANGE_TOK + last_fill).astype(jnp.int32)
    positions = jnp.arange(TOTAL_SLOTS, dtype=jnp.int32)
    inverse = jnp.zeros((TOTAL_SLOTS,), jnp.int32).at[slot_table].set(positions)
    slot_row = jnp.sum((inverse[:, None] >= inclusive[None, :]).astype(jnp.int32), axis=1).astype(jnp.int32)
    slot_range = (inverse - exclusive[slot_row]).astype(jnp.int32)
    slot_len = lengths[slot_row]
    grouped = query.reshape(ROWS, KVH, GROUP, HD)
    token_index = jnp.arange(RANGE_TOK, dtype=jnp.int32)
    scaling = HD ** -0.5

    def one_slot(packed_codes):
        key_rows, value_rows, key_page_scale, value_page_scale, row_index, range_index, length_valid = packed_codes
        queries = grouped[row_index]
        dotted = jnp.einsum('kgd,ktd->kgt', queries.astype(jnp.float32), key_rows.astype(jnp.float32))
        key_token_rows = jnp.repeat(key_page_scale, PAGE_TOKENS, axis=-1)
        scores = dotted * key_token_rows[:, None, :] * scaling
        live = range_index * RANGE_TOK + token_index < length_valid
        scores = jnp.where(live[None, None, :], scores, -jnp.inf)
        maxima = jnp.max(scores, axis=-1)
        expons = jnp.exp(scores - maxima[..., None])
        totals = jnp.sum(expons, axis=-1)
        value_tok = jnp.repeat(value_page_scale, PAGE_TOKENS, axis=-1)
        weights = (expons * value_tok[:, None, :]).astype(jnp.bfloat16)
        partial_out = jnp.einsum('kgt,ktd->kgd', weights.astype(jnp.float32), value_rows.astype(jnp.float32))
        return maxima.reshape(QH), totals.reshape(QH), partial_out.reshape(QH, HD)

    maxima, totals, partial_out = lax.map(one_slot, (key_codes, value_codes, key_scale, value_scale, slot_row, slot_range, slot_len))
    row_ids = jnp.arange(ROWS, dtype=jnp.int32)
    highest = jnp.max(jnp.where(slot_row[None, :, None] == row_ids[:, None, None], maxima[None], -jnp.inf), axis=1)
    factor = jnp.exp(maxima - highest[slot_row])
    numerator = jax.ops.segment_sum(factor[..., None] * partial_out, slot_row, num_segments=ROWS)
    denominator = jax.ops.segment_sum(factor * totals, slot_row, num_segments=ROWS)
    attention = (numerator / denominator[..., None]).reshape(ROWS, QH * HD).astype(jnp.bfloat16)
    return jnp.dot(attention, out_weight, preferred_element_type=jnp.float32).astype(jnp.bfloat16)
```

```python
import functools

import jax
import jax.numpy as jnp
from jax import lax
from jax.experimental import pallas as pl
from jax.experimental.pallas import tpu as pltpu
from jax.sharding import PartitionSpec as P

LANES = 128
LOW = -1e30
MIB = 1 << 20
VMEM = pl.BlockSpec(memory_space=pltpu.VMEM)
SMEM = pl.BlockSpec(memory_space=pltpu.SMEM)


def exchange_rounds(devices):
    rounds, width = [], devices
    while width > 1:
        radix = 4 if width % 4 == 0 else 2
        width //= radix
        rounds.append([width * k for k in range(1, radix)])
    return rounds


def partner(value, mask, devices):
    return lax.ppermute(value, "page", [(i, i ^ mask) for i in range(devices)])


def stat_place(piece, entries):
    each = LANES // entries
    return piece // each, (piece % each) * entries


def stat_blocks(entries):
    return stat_place(2, entries)[0] + 1


def lane_index(shape):
    return lax.broadcasted_iota(jnp.int32, shape, 1)


def store_stats(out_ref, base, logs, entries, heads):
    high = logs.astype(jnp.bfloat16).astype(jnp.float32)
    middle = (logs - high).astype(jnp.bfloat16).astype(jnp.float32)
    low = logs - high - middle
    lane = lane_index((heads, LANES))
    blocks = [jnp.zeros((heads, LANES), jnp.float32) for _ in range(stat_blocks(entries))]
    for piece, value in enumerate((high, middle, low)):
        block, offset = stat_place(piece, entries)
        moved = pltpu.roll(value, offset, 1) if offset else value
        inside = (lane >= offset) & (lane < offset + entries)
        blocks[block] = jnp.where(inside, moved, blocks[block])
    table = jnp.concatenate(blocks, axis=0) if len(blocks) > 1 else blocks[0]
    out_ref[base : base + table.shape[0], :] = table.astype(jnp.bfloat16)


def load_stats(ref, base, entries, heads):
    rows = stat_blocks(entries) * heads
    table = ref[base : base + rows, :].astype(jnp.float32)
    total = None
    for piece in range(3):
        block, offset = stat_place(piece, entries)
        value = table[block * heads : (block + 1) * heads]
        value = pltpu.roll(value, LANES - offset, 1) if offset else value
        total = value if total is None else total + value
    return total


def load_entry(ref, index, heads):
    if heads % 16 == 0:
        return ref[index * heads : (index + 1) * heads, :].astype(jnp.float32)
    base = index * heads // 16 * 16
    block = ref[base : base + 16, :].astype(jnp.float32)
    return block[index * heads - base : (index + 1) * heads - base]


def attend_kernel(
    pieces, slots, kv_heads, group, tokens, pages, key_scaling,
    place_ref, live_ref, key_scale_ref, value_scale_ref, *refs,
):
    query_refs = refs[:pieces]
    key_ref, value_ref, out_ref, queries, outs = refs[pieces:]
    heads = kv_heads * group
    page_tokens = tokens // pages
    held = query_refs[0].shape[0]
    for piece, query_ref in enumerate(query_refs):
        block = query_ref[...].astype(jnp.float32)
        for head in range(heads):
            queries[pl.ds(piece * held * heads + head, held, stride=heads), :] = block[
                :, head * LANES : (head + 1) * LANES
            ]
    together = 2 if kv_heads % 2 == 0 else 1
    rows = together * group
    lane = lane_index((heads, LANES))
    logs = jnp.zeros((heads, LANES), jnp.float32)
    for slot in range(slots):
        start = pl.multiple_of(place_ref[slot] * heads, 8)
        query = queries[pl.ds(start, heads), :].astype(jnp.bfloat16)
        live = live_ref[slot]
        column = []
        for first in range(0, kv_heads, together):
            own = query[first * group : first * group + rows]
            if together == 2:
                upper = lax.broadcasted_iota(jnp.int32, (rows, LANES), 0) < group
                zero = jnp.zeros_like(own)
                own = jnp.concatenate(
                    [jnp.where(upper, own, zero), jnp.where(upper, zero, own)], axis=1
                )
                keys = jnp.concatenate([key_ref[slot, first], key_ref[slot, first + 1]], axis=1)
                values = jnp.concatenate(
                    [value_ref[slot, first], value_ref[slot, first + 1]], axis=1
                )
            else:
                keys, values = key_ref[slot, first], value_ref[slot, first]
            dotted = lax.dot_general(
                own, keys, (((1,), (1,)), ((), ())), preferred_element_type=jnp.float32
            )

            def by_page(scale_ref, page):
                parts = [
                    jnp.full((group, page_tokens), scale_ref[slot, first + k, page], jnp.float32)
                    for k in range(together)
                ]
                return jnp.concatenate(parts, axis=0) if together > 1 else parts[0]

            token = lane_index((rows, page_tokens))
            scores = []
            for page in range(pages):
                part = dotted[:, page * page_tokens : (page + 1) * page_tokens]
                part = part * (by_page(key_scale_ref, page) * key_scaling)
                scores.append(jnp.where(token + page * page_tokens < live, part, LOW))
            peak = functools.reduce(jnp.maximum, scores)
            peak = jnp.max(peak, axis=1, keepdims=True)
            total = None
            weights = []
            for page in range(pages):
                expon = jnp.exp(scores[page] - peak)
                total = expon if total is None else total + expon
                weights.append((expon * by_page(value_scale_ref, page)).astype(jnp.bfloat16))
            total = jnp.sum(total, axis=1, keepdims=True)
            partial = jnp.dot(
                jnp.concatenate(weights, axis=1), values, preferred_element_type=jnp.float32
            )
            if together == 2:
                partial = jnp.concatenate(
                    [partial[:group, :LANES], partial[group:, LANES:]], axis=0
                )
            at = slot * heads + first * group
            outs[at : at + rows, :] = partial / total
            column.append(peak + jnp.log(total))
        column = jnp.concatenate(column, axis=0) if len(column) > 1 else column[0]
        logs = jnp.where(lane == slot, column, logs)
    out_ref[: slots * heads, :] = outs[...].astype(jnp.bfloat16)
    store_stats(out_ref, slots * heads, logs, slots, heads)


def merge_slots_kernel(groups, slots, rows, heads, owner_ref, owner_lane_ref, *refs):
    out_ref, sums = refs[groups:]
    lane = lane_index((heads, LANES))
    owner = jnp.broadcast_to(owner_lane_ref[...], (heads, LANES))
    logs = jnp.full((heads, LANES), LOW, jnp.float32)
    for index in range(groups):
        own = load_stats(refs[index], slots * heads, slots, heads)
        own = pltpu.roll(own, index * slots, 1) if index else own
        inside = (lane >= index * slots) & (lane < (index + 1) * slots)
        logs = jnp.where(inside, own, logs)
    tops = jnp.zeros((heads, LANES), jnp.float32)
    row_top = []
    for row in range(rows):
        top = jnp.max(jnp.where(owner == row, logs, LOW), axis=1, keepdims=True)
        tops = jnp.where(owner == row, top, tops)
        row_top.append(top)
    factor = jnp.exp(logs - tops)
    totals = jnp.ones((heads, LANES), jnp.float32)
    row_logs = jnp.full((heads, LANES), LOW, jnp.float32)
    for row in range(rows):
        total = jnp.sum(jnp.where(owner == row, factor, 0.0), axis=1, keepdims=True)
        totals = jnp.where(owner == row, total, totals)
        held = total > 0.0
        value = jnp.where(held, row_top[row] + jnp.log(jnp.where(held, total, 1.0)), LOW)
        row_logs = jnp.where(lane == row, value, row_logs)
    weight = factor / totals
    sums[...] = jnp.zeros_like(sums)
    for index in range(groups):
        for slot in range(slots):
            at = index * slots + slot
            start = pl.multiple_of(owner_ref[at] * heads, 8)
            block = pl.ds(start, heads)
            sums[block, :] += weight[:, at : at + 1] * load_entry(refs[index], slot, heads)
    out_ref[: rows * heads, :] = sums[...].astype(jnp.bfloat16)
    store_stats(out_ref, rows * heads, row_logs, rows, heads)


def merge_rows(refs, rows, heads, sums):
    logs = [load_stats(ref, rows * heads, rows, heads) for ref in refs]
    top = functools.reduce(jnp.maximum, logs)
    factors = [jnp.exp(log - top) for log in logs]
    total = functools.reduce(jnp.add, factors)
    weights = [factor / total for factor in factors]
    for row in range(rows):
        parts = [
            weight[:, row : row + 1] * load_entry(ref, row, heads)
            for weight, ref in zip(weights, refs)
        ]
        sums[row * heads : (row + 1) * heads, :] = functools.reduce(jnp.add, parts)
    return top + jnp.log(total)


def merge_rows_kernel(groups, rows, heads, *refs):
    out_ref, sums = refs[groups:]
    logs = merge_rows(refs[:groups], rows, heads, sums)
    out_ref[: rows * heads, :] = sums[...].astype(jnp.bfloat16)
    store_stats(out_ref, rows * heads, logs, rows, heads)


def project_kernel(groups, rows, heads, *refs):
    weight_ref, out_ref, sums = refs[groups:]
    merge_rows(refs[:groups], rows, heads, sums)
    attention = jnp.concatenate(
        [sums[pl.ds(head, rows, stride=heads), :].astype(jnp.bfloat16) for head in range(heads)],
        axis=1,
    )
    out_ref[...] = jnp.dot(attention, weight_ref[...], preferred_element_type=jnp.float32)


def per_device(
    query,
    key_codes,
    value_codes,
    key_scale,
    value_scale,
    out_weight,
    range_counts,
    last_fill,
    slot_table,
    *,
    devices,
    head_devices,
):
    slots, kv_heads, tokens, head_dim = key_codes.shape
    pages = key_scale.shape[2]
    rows = range_counts.shape[0]
    all_slots = slot_table.shape[0]
    heads = query.shape[1] // head_dim
    group = heads // kv_heads
    own_rows = query.shape[0]
    columns = out_weight.shape[1]
    rounds = exchange_rounds(devices)
    me = lax.axis_index("page")

    inclusive = jnp.cumsum(range_counts)
    lengths = (range_counts - 1) * tokens + last_fill
    slot_ids = jnp.arange(all_slots, dtype=jnp.int32)
    inverse = jnp.sum(
        jnp.where(slot_table[None, :] == slot_ids[:, None], slot_ids[None, :], 0), axis=1
    )
    slot_row = jnp.sum((inverse[:, None] >= inclusive[None, :]).astype(jnp.int32), axis=1)
    picked = slot_row[:, None] == jnp.arange(rows, dtype=jnp.int32)[None, :]
    slot_end = jnp.sum(
        jnp.where(picked, (lengths + (inclusive - range_counts) * tokens)[None, :], 0), axis=1
    )
    slot_live = slot_end - inverse * tokens

    order = [0]
    held = [query]
    for masks in rounds:
        block = jnp.concatenate(held, axis=0) if len(held) > 1 else held[0]
        held = [block] + [partner(block, mask, devices) for mask in masks]
        order = [mask ^ old for mask in [0] + masks for old in order]
    place_of = [0] * devices
    for place, mask in enumerate(order):
        place_of[mask] = place
    own_slots = lax.dynamic_slice(slot_row, (me * slots,), (slots,))
    own_live = lax.dynamic_slice(slot_live, (me * slots,), (slots,))
    away = jnp.bitwise_xor(own_slots // own_rows, me)
    place = jnp.sum(
        jnp.where(
            away[:, None] == jnp.arange(devices, dtype=jnp.int32)[None, :],
            jnp.array(place_of, jnp.int32)[None, :],
            0,
        ),
        axis=1,
    )
    place = place * own_rows + own_slots % own_rows

    payload = (slots + stat_blocks(slots)) * heads
    held = [
        pl.pallas_call(
            functools.partial(
                attend_kernel, len(held), slots, kv_heads, group, tokens, pages, head_dim**-0.5
            ),
            out_shape=jax.ShapeDtypeStruct((payload, LANES), jnp.bfloat16),
            in_specs=[SMEM] * 4 + [VMEM] * (len(held) + 2),
            out_specs=VMEM,
            scratch_shapes=[
                pltpu.VMEM((rows * heads, LANES), jnp.float32),
                pltpu.VMEM((slots * heads, LANES), jnp.float32),
            ],
            compiler_params=pltpu.CompilerParams(vmem_limit_bytes=24 * MIB),
            name="attend",
        )(place, own_live, key_scale, value_scale, *held, key_codes, value_codes)
    ]

    payload = (rows + stat_blocks(rows)) * heads
    sums = pltpu.VMEM((rows * heads, LANES), jnp.float32)
    for turn, masks in enumerate(rounds):
        held = held + [partner(held[0], mask, devices) for mask in masks]
        groups = len(held)
        params = pltpu.CompilerParams(vmem_limit_bytes=16 * MIB)
        if turn == 0:
            sources = [me] + [jnp.bitwise_xor(me, mask) for mask in masks]
            owner = jnp.concatenate(
                [lax.dynamic_slice(slot_row, (source * slots,), (slots,)) for source in sources]
            )
            owner_lane = jnp.full((1, LANES), -1, jnp.int32).at[0, : groups * slots].set(owner)
            held = [
                pl.pallas_call(
                    functools.partial(merge_slots_kernel, groups, slots, rows, heads),
                    out_shape=jax.ShapeDtypeStruct((payload, LANES), jnp.bfloat16),
                    in_specs=[SMEM] + [VMEM] * (groups + 1),
                    out_specs=VMEM,
                    scratch_shapes=[sums],
                    compiler_params=params,
                    name="merge_slots",
                )(owner, owner_lane, *held)
            ]
        elif turn < len(rounds) - 1:
            held = [
                pl.pallas_call(
                    functools.partial(merge_rows_kernel, groups, rows, heads),
                    out_shape=jax.ShapeDtypeStruct((payload, LANES), jnp.bfloat16),
                    in_specs=[VMEM] * groups,
                    out_specs=VMEM,
                    scratch_shapes=[sums],
                    compiler_params=params,
                    name="merge_rows",
                )(*held)
            ]
    mixed = pl.pallas_call(
        functools.partial(project_kernel, len(held), rows, heads),
        out_shape=jax.ShapeDtypeStruct((rows, columns), jnp.float32),
        in_specs=[VMEM] * (len(held) + 1),
        out_specs=VMEM,
        scratch_shapes=[sums],
        compiler_params=pltpu.CompilerParams(vmem_limit_bytes=16 * MIB),
        name="project",
    )(*held, out_weight)
    if head_devices == 2:
        half = rows // 2
        side = lax.axis_index("head")
        keep = lax.dynamic_slice(mixed, (side * half, 0), (half, columns))
        give = lax.dynamic_slice(mixed, ((1 - side) * half, 0), (half, columns))
        mixed = keep + lax.ppermute(give, "head", [(0, 1), (1, 0)])
    else:
        mixed = lax.psum_scatter(mixed, "head", scatter_dimension=0, tiled=True)
    return mixed.astype(jnp.bfloat16)


def solution(mesh):
    return jax.shard_map(
        functools.partial(
            per_device, devices=mesh.shape["page"], head_devices=mesh.shape["head"]
        ),
        mesh=mesh,
        in_specs=(
            P("page", "head"),
            P("page", "head", None, None),
            P("page", "head", None, None),
            P("page", "head", None),
            P("page", "head", None),
            P("head", "page"),
            P(),
            P(),
            P(),
        ),
        out_specs=P("head", "page"),
        check_vma=False,
    )
```

```python
import functools

import jax
import jax.numpy as jnp
from jax import lax
from jax.experimental import pallas as pl
from jax.experimental.pallas import tpu as pltpu
from jax.sharding import PartitionSpec as P

LANES = 128
LOW = -1e30
LOCATE_FLOPS = 20_000_000_000
ATTEND_FLOPS = 5_000_000_000
MERGE_FLOPS = 20_000_000_000
MIB = 1 << 20
VMEM = pl.BlockSpec(memory_space=pltpu.VMEM)
SMEM = pl.BlockSpec(memory_space=pltpu.SMEM)


def exchange_rounds(devices, most):
    rounds, width = [], devices
    while width > 1:
        radix = most if width % most == 0 else 2
        width //= radix
        rounds.append([width * k for k in range(1, radix)])
    return rounds


def partner(value, mask, devices):
    return lax.ppermute(value, "page", [(i, i ^ mask) for i in range(devices)])


def stat_place(piece, entries):
    each = LANES // entries
    return piece // each, (piece % each) * entries


def stat_blocks(entries):
    return stat_place(2, entries)[0] + 1


def lane_index(shape):
    return lax.broadcasted_iota(jnp.int32, shape, 1)


def store_stats(out_ref, base, logs, entries, heads):
    high = logs.astype(jnp.bfloat16).astype(jnp.float32)
    middle = (logs - high).astype(jnp.bfloat16).astype(jnp.float32)
    low = logs - high - middle
    lane = lane_index((heads, LANES))
    blocks = [jnp.zeros((heads, LANES), jnp.float32) for _ in range(stat_blocks(entries))]
    for piece, value in enumerate((high, middle, low)):
        block, offset = stat_place(piece, entries)
        moved = pltpu.roll(value, offset, 1) if offset else value
        inside = (lane >= offset) & (lane < offset + entries)
        blocks[block] = jnp.where(inside, moved, blocks[block])
    table = jnp.concatenate(blocks, axis=0) if len(blocks) > 1 else blocks[0]
    out_ref[base : base + table.shape[0], :] = table.astype(jnp.bfloat16)


def load_stats(ref, base, entries, heads):
    rows = stat_blocks(entries) * heads
    table = ref[base : base + rows, :].astype(jnp.float32)
    total = None
    for piece in range(3):
        block, offset = stat_place(piece, entries)
        value = table[block * heads : (block + 1) * heads]
        value = pltpu.roll(value, LANES - offset, 1) if offset else value
        total = value if total is None else total + value
    return total


def load_entry(ref, index, heads):
    if heads % 16 == 0:
        return ref[index * heads : (index + 1) * heads, :].astype(jnp.float32)
    base = index * heads // 16 * 16
    block = ref[base : base + 16, :].astype(jnp.float32)
    return block[index * heads - base : (index + 1) * heads - base]


def locate_kernel(
    rounds, near, slots, rows, all_slots, own_rows, tokens,
    table_ref, place_ref, live_ref, owner_ref, position_of, first_of,
):
    me = lax.axis_index("page")
    fills, entries = rows, 2 * rows

    def note(position, carry):
        position_of[table_ref[entries + position]] = position
        return carry

    lax.fori_loop(0, all_slots, note, 0, unroll=16)
    ends, end = [], jnp.int32(0)
    for row in range(rows):
        first_of[row] = end
        end = end + table_ref[row]
        ends.append(end)
    for index, mask in enumerate(near):
        source = jnp.bitwise_xor(me, mask)
        for slot in range(slots):
            position = position_of[source * slots + slot]
            row = functools.reduce(
                jnp.add, [(position >= end).astype(jnp.int32) for end in ends[:-1]]
            )
            owner_ref[index * slots + slot] = row
            if index == 0:
                away = jnp.bitwise_xor(row // own_rows, me)
                place, step_size = row % own_rows, own_rows
                for masks in rounds:
                    radix = len(masks) + 1
                    place += away // masks[0] % radix * step_size
                    step_size *= radix
                place_ref[slot] = place
                before = position - first_of[row]
                live_ref[slot] = (table_ref[row] - 1 - before) * tokens + table_ref[fills + row]


def attend_kernel(
    pieces, slots, kv_heads, group, tokens, pages, key_scaling,
    place_ref, live_ref, key_scale_ref, value_scale_ref, *refs,
):
    query_refs = refs[:pieces]
    key_ref, value_ref, out_ref, queries, outs = refs[pieces:]
    heads = kv_heads * group
    page_tokens = tokens // pages
    held = query_refs[0].shape[0]
    for piece, query_ref in enumerate(query_refs):
        block = query_ref[...].astype(jnp.float32)
        for head in range(heads):
            queries[pl.ds(piece * held * heads + head, held, stride=heads), :] = block[
                :, head * LANES : (head + 1) * LANES
            ]
    together = 2 if kv_heads % 2 == 0 else 1
    rows = together * group
    lane = lane_index((heads, LANES))
    logs = jnp.zeros((heads, LANES), jnp.float32)
    for slot in range(slots):
        start = pl.multiple_of(place_ref[slot] * heads, 8)
        query = queries[pl.ds(start, heads), :].astype(jnp.bfloat16)
        live = live_ref[slot]
        column = []
        for first in range(0, kv_heads, together):
            own = query[first * group : first * group + rows]
            if together == 2:
                upper = lax.broadcasted_iota(jnp.int32, (rows, LANES), 0) < group
                zero = jnp.zeros_like(own)
                own = jnp.concatenate(
                    [jnp.where(upper, own, zero), jnp.where(upper, zero, own)], axis=1
                )
                keys = jnp.concatenate([key_ref[slot, first], key_ref[slot, first + 1]], axis=1)
                values = jnp.concatenate(
                    [value_ref[slot, first], value_ref[slot, first + 1]], axis=1
                )
            else:
                keys, values = key_ref[slot, first], value_ref[slot, first]
            dotted = lax.dot_general(
                own, keys, (((1,), (1,)), ((), ())), preferred_element_type=jnp.float32
            )

            def by_page(scale_ref, page):
                parts = [
                    jnp.full((group, page_tokens), scale_ref[slot, first + k, page], jnp.float32)
                    for k in range(together)
                ]
                return jnp.concatenate(parts, axis=0) if together > 1 else parts[0]

            token = lane_index((rows, page_tokens))
            scores = []
            for page in range(pages):
                part = dotted[:, page * page_tokens : (page + 1) * page_tokens]
                part = part * (by_page(key_scale_ref, page) * key_scaling)
                scores.append(jnp.where(token + page * page_tokens < live, part, LOW))
            peak = functools.reduce(jnp.maximum, scores)
            peak = jnp.max(peak, axis=1, keepdims=True)
            total = None
            weights = []
            for page in range(pages):
                expon = jnp.exp(scores[page] - peak)
                total = expon if total is None else total + expon
                weights.append((expon * by_page(value_scale_ref, page)).astype(jnp.bfloat16))
            total = jnp.sum(total, axis=1, keepdims=True)
            partial = jnp.dot(
                jnp.concatenate(weights, axis=1), values, preferred_element_type=jnp.float32
            )
            if together == 2:
                partial = jnp.concatenate(
                    [partial[:group, :LANES], partial[group:, LANES:]], axis=0
                )
            at = slot * heads + first * group
            outs[at : at + rows, :] = partial / total
            column.append(peak + jnp.log(total))
        column = jnp.concatenate(column, axis=0) if len(column) > 1 else column[0]
        logs = jnp.where(lane == slot, column, logs)
    out_ref[: slots * heads, :] = outs[...].astype(jnp.bfloat16)
    store_stats(out_ref, slots * heads, logs, slots, heads)


def merge_slots_kernel(groups, slots, rows, heads, owner_ref, *refs):
    out_ref, sums = refs[groups:]
    lane = lane_index((heads, LANES))
    owner = jnp.full((8, LANES), -1, jnp.int32)
    for at in range(groups * slots):
        owner = jnp.where(lane[:8] == at, owner_ref[at], owner)
    owner = jnp.concatenate([owner] * (heads // 8), axis=0)
    logs = jnp.full((heads, LANES), LOW, jnp.float32)
    for index in range(groups):
        own = load_stats(refs[index], slots * heads, slots, heads)
        own = pltpu.roll(own, index * slots, 1) if index else own
        inside = (lane >= index * slots) & (lane < (index + 1) * slots)
        logs = jnp.where(inside, own, logs)
    tops = jnp.zeros((heads, LANES), jnp.float32)
    row_top = []
    for row in range(rows):
        top = jnp.max(jnp.where(owner == row, logs, LOW), axis=1, keepdims=True)
        tops = jnp.where(owner == row, top, tops)
        row_top.append(top)
    factor = jnp.exp(logs - tops)
    totals = jnp.ones((heads, LANES), jnp.float32)
    row_logs = jnp.full((heads, LANES), LOW, jnp.float32)
    for row in range(rows):
        total = jnp.sum(jnp.where(owner == row, factor, 0.0), axis=1, keepdims=True)
        totals = jnp.where(owner == row, total, totals)
        held = total > 0.0
        value = jnp.where(held, row_top[row] + jnp.log(jnp.where(held, total, 1.0)), LOW)
        row_logs = jnp.where(lane == row, value, row_logs)
    weight = factor / totals
    sums[...] = jnp.zeros_like(sums)
    for index in range(groups):
        for slot in range(slots):
            at = index * slots + slot
            start = pl.multiple_of(owner_ref[at] * heads, 8)
            block = pl.ds(start, heads)
            sums[block, :] += weight[:, at : at + 1] * load_entry(refs[index], slot, heads)
    out_ref[: rows * heads, :] = sums[...].astype(jnp.bfloat16)
    store_stats(out_ref, rows * heads, row_logs, rows, heads)


def merge_rows(refs, rows, heads, sums):
    logs = [load_stats(ref, rows * heads, rows, heads) for ref in refs]
    top = functools.reduce(jnp.maximum, logs)
    factors = [jnp.exp(log - top) for log in logs]
    total = functools.reduce(jnp.add, factors)
    weights = [factor / total for factor in factors]
    for row in range(rows):
        parts = [
            weight[:, row : row + 1] * load_entry(ref, row, heads)
            for weight, ref in zip(weights, refs)
        ]
        sums[row * heads : (row + 1) * heads, :] = functools.reduce(jnp.add, parts)
    return top + jnp.log(total)


def merge_rows_kernel(groups, rows, heads, *refs):
    out_ref, sums = refs[groups:]
    logs = merge_rows(refs[:groups], rows, heads, sums)
    out_ref[: rows * heads, :] = sums[...].astype(jnp.bfloat16)
    store_stats(out_ref, rows * heads, logs, rows, heads)


def project_kernel(groups, rows, heads, halves, *refs):
    weight_ref, *out_refs, sums = refs[groups:]
    merge_rows(refs[:groups], rows, heads, sums)
    attention = jnp.concatenate(
        [sums[pl.ds(head, rows, stride=heads), :].astype(jnp.bfloat16) for head in range(heads)],
        axis=1,
    )
    mixed = jnp.dot(attention, weight_ref[...], preferred_element_type=jnp.float32)
    if halves:
        first = lax.axis_index("head") == 0
        lower, upper = mixed[: rows // 2], mixed[rows // 2 :]
        out_refs[0][...] = jnp.where(first, lower, upper)
        out_refs[1][...] = jnp.where(first, upper, lower)
    else:
        out_refs[0][...] = mixed


def per_device(
    query,
    key_codes,
    value_codes,
    key_scale,
    value_scale,
    out_weight,
    range_counts,
    last_fill,
    slot_table,
    *,
    devices,
    head_devices,
):
    slots, kv_heads, tokens, head_dim = key_codes.shape
    pages = key_scale.shape[2]
    rows = range_counts.shape[0]
    all_slots = slot_table.shape[0]
    heads = query.shape[1] // head_dim
    group = heads // kv_heads
    own_rows = query.shape[0]
    columns = out_weight.shape[1]
    spread = exchange_rounds(devices, 2)
    rounds = exchange_rounds(devices, 4)

    near = [0] + rounds[0]
    own_slots = jax.ShapeDtypeStruct((slots,), jnp.int32)
    place, live, owner = pl.pallas_call(
        functools.partial(
            locate_kernel, spread, near, slots, rows, all_slots, own_rows, tokens
        ),
        out_shape=[own_slots, own_slots, jax.ShapeDtypeStruct((len(near) * slots,), jnp.int32)],
        in_specs=[SMEM],
        out_specs=[SMEM] * 3,
        scratch_shapes=[
            pltpu.SMEM((all_slots,), jnp.int32),
            pltpu.SMEM((rows,), jnp.int32),
        ],
        cost_estimate=pl.CostEstimate(
            flops=LOCATE_FLOPS, bytes_accessed=4 * all_slots, transcendentals=0
        ),
        compiler_params=pltpu.CompilerParams(vmem_limit_bytes=MIB),
        name="locate",
    )(jnp.concatenate([range_counts, last_fill, slot_table]))

    held = [query]
    for turn, masks in enumerate(spread):
        block = jnp.concatenate(held, axis=0) if len(held) > 1 else held[0]
        if turn == 1:
            block, place, live, owner = lax.optimization_barrier((block, place, live, owner))
        elif turn > 1:
            block = lax.optimization_barrier(block)
        held = [block] + [partner(block, mask, devices) for mask in masks]

    payload = (slots + stat_blocks(slots)) * heads
    held = [
        pl.pallas_call(
            functools.partial(
                attend_kernel, len(held), slots, kv_heads, group, tokens, pages, head_dim**-0.5
            ),
            out_shape=jax.ShapeDtypeStruct((payload, LANES), jnp.bfloat16),
            in_specs=[SMEM] * 4 + [VMEM] * (len(held) + 2),
            out_specs=VMEM,
            scratch_shapes=[
                pltpu.VMEM((rows * heads, LANES), jnp.float32),
                pltpu.VMEM((slots * heads, LANES), jnp.float32),
            ],
            compiler_params=pltpu.CompilerParams(vmem_limit_bytes=8 * MIB),
            cost_estimate=pl.CostEstimate(
                flops=ATTEND_FLOPS,
                bytes_accessed=4 * slots * kv_heads * tokens * head_dim,
                transcendentals=slots * heads * tokens,
            ),
            name="attend",
        )(place, live, key_scale, value_scale, *held, key_codes, value_codes)
    ]

    payload = (rows + stat_blocks(rows)) * heads
    sums = pltpu.VMEM((rows * heads, LANES), jnp.float32)
    for turn, masks in enumerate(rounds):
        held = held + [partner(held[0], mask, devices) for mask in masks]
        groups = len(held)
        params = pltpu.CompilerParams(vmem_limit_bytes=8 * MIB)
        if turn == 0:
            held = [
                pl.pallas_call(
                    functools.partial(merge_slots_kernel, groups, slots, rows, heads),
                    out_shape=jax.ShapeDtypeStruct((payload, LANES), jnp.bfloat16),
                    in_specs=[SMEM] + [VMEM] * groups,
                    out_specs=VMEM,
                    scratch_shapes=[sums],
                    compiler_params=params,
                    cost_estimate=pl.CostEstimate(
                        flops=MERGE_FLOPS, bytes_accessed=2 * payload * LANES, transcendentals=0
                    ),
                    name="merge_slots",
                )(owner, *held)
            ]
        elif turn < len(rounds) - 1:
            held = [
                pl.pallas_call(
                    functools.partial(merge_rows_kernel, groups, rows, heads),
                    out_shape=jax.ShapeDtypeStruct((payload, LANES), jnp.bfloat16),
                    in_specs=[VMEM] * groups,
                    out_specs=VMEM,
                    scratch_shapes=[sums],
                    compiler_params=params,
                    name="merge_rows",
                )(*held)
            ]
    halves = head_devices == 2
    mixed_shape = jax.ShapeDtypeStruct((rows // (1 + halves), columns), jnp.float32)
    mixed, *give = pl.pallas_call(
        functools.partial(project_kernel, len(held), rows, heads, halves),
        out_shape=[mixed_shape] * (1 + halves),
        in_specs=[VMEM] * (len(held) + 1),
        out_specs=[VMEM] * (1 + halves),
        scratch_shapes=[sums],
        compiler_params=pltpu.CompilerParams(vmem_limit_bytes=8 * MIB),
        name="project",
    )(*held, out_weight)
    if halves:
        mixed = mixed + lax.ppermute(give[0], "head", [(0, 1), (1, 0)])
    else:
        mixed = lax.psum_scatter(mixed, "head", scatter_dimension=0, tiled=True)
    return mixed.astype(jnp.bfloat16)


def solution(mesh):
    return jax.shard_map(
        functools.partial(
            per_device, devices=mesh.shape["page"], head_devices=mesh.shape["head"]
        ),
        mesh=mesh,
        in_specs=(
            P("page", "head"),
            P("page", "head", None, None),
            P("page", "head", None, None),
            P("page", "head", None),
            P("page", "head", None),
            P("head", "page"),
            P(),
            P(),
            P(),
        ),
        out_specs=P("head", "page"),
        check_vma=False,
    )
```

```python
import functools

import jax
import jax.numpy as jnp
from jax import lax
from jax.experimental import pallas as pl
from jax.experimental.pallas import tpu as pltpu
from jax.sharding import PartitionSpec as P

LANES = 128
LOW = -1e30
LOCATE_FLOPS = 20_000_000_000
ATTEND_FLOPS = 5_000_000_000
MERGE_FLOPS = 20_000_000_000
MIB = 1 << 20
VMEM = pl.BlockSpec(memory_space=pltpu.VMEM)
SMEM = pl.BlockSpec(memory_space=pltpu.SMEM)


def exchange_rounds(devices, most):
    rounds, width = [], devices
    while width > 1:
        radix = most if width % most == 0 else 2
        width //= radix
        rounds.append([width * k for k in range(1, radix)])
    return rounds


def partner(value, mask, devices):
    return lax.ppermute(value, "page", [(i, i ^ mask) for i in range(devices)])


def stat_place(piece, entries):
    each = LANES // entries
    return piece // each, (piece % each) * entries


def stat_blocks(entries):
    return stat_place(2, entries)[0] + 1


def lane_index(shape):
    return lax.broadcasted_iota(jnp.int32, shape, 1)


def store_stats(out_ref, base, logs, entries, heads):
    high = logs.astype(jnp.bfloat16).astype(jnp.float32)
    middle = (logs - high).astype(jnp.bfloat16).astype(jnp.float32)
    low = logs - high - middle
    lane = lane_index((heads, LANES))
    blocks = [jnp.zeros((heads, LANES), jnp.float32) for _ in range(stat_blocks(entries))]
    for piece, value in enumerate((high, middle, low)):
        block, offset = stat_place(piece, entries)
        moved = pltpu.roll(value, offset, 1) if offset else value
        inside = (lane >= offset) & (lane < offset + entries)
        blocks[block] = jnp.where(inside, moved, blocks[block])
    table = jnp.concatenate(blocks, axis=0) if len(blocks) > 1 else blocks[0]
    out_ref[base : base + table.shape[0], :] = table.astype(jnp.bfloat16)


def load_stats(ref, base, entries, heads):
    rows = stat_blocks(entries) * heads
    table = ref[base : base + rows, :].astype(jnp.float32)
    total = None
    for piece in range(3):
        block, offset = stat_place(piece, entries)
        value = table[block * heads : (block + 1) * heads]
        value = pltpu.roll(value, LANES - offset, 1) if offset else value
        total = value if total is None else total + value
    return total


def load_entry(ref, index, heads):
    if heads % 16 == 0:
        return ref[index * heads : (index + 1) * heads, :].astype(jnp.float32)
    base = index * heads // 16 * 16
    block = ref[base : base + 16, :].astype(jnp.float32)
    return block[index * heads - base : (index + 1) * heads - base]


def locate_kernel(
    rounds, near, slots, rows, all_slots, own_rows, tokens,
    table_ref, place_ref, live_ref, owner_ref, position_of, first_of,
):
    me = lax.axis_index("page")
    fills, entries = rows, 2 * rows

    def note(position, carry):
        position_of[table_ref[entries + position]] = position
        return carry

    lax.fori_loop(0, all_slots, note, 0, unroll=16)
    ends, end = [], jnp.int32(0)
    for row in range(rows):
        first_of[row] = end
        end = end + table_ref[row]
        ends.append(end)
    for index, mask in enumerate(near):
        source = jnp.bitwise_xor(me, mask)
        for slot in range(slots):
            position = position_of[source * slots + slot]
            row = functools.reduce(
                jnp.add, [(position >= end).astype(jnp.int32) for end in ends[:-1]]
            )
            owner_ref[index * slots + slot] = row
            if index == 0:
                away = jnp.bitwise_xor(row // own_rows, me)
                place, step_size = row % own_rows, own_rows
                for masks in rounds:
                    radix = len(masks) + 1
                    place += away // masks[0] % radix * step_size
                    step_size *= radix
                place_ref[slot] = place
                before = position - first_of[row]
                live_ref[slot] = (table_ref[row] - 1 - before) * tokens + table_ref[fills + row]


def columns_kernel(group, factor, *refs):
    for scale_ref, out_ref, multiplier in zip(refs[:2], refs[2:], (factor, 1.0)):
        slots, kv_heads, pages = scale_ref.shape
        batches = out_ref.shape[0]
        each = slots // batches
        for batch in range(batches):
            parts = []
            for index in range(each):
                scale = scale_ref[batch * each + index] * multiplier
                for kv in range(kv_heads):
                    parts.append(jnp.broadcast_to(scale[kv : kv + 1], (group, pages)))
            table = jnp.concatenate(parts, axis=0)
            for page in range(pages):
                out_ref[batch, page] = jnp.broadcast_to(
                    table[:, page : page + 1], (table.shape[0], LANES)
                )


def attend_kernel(
    pieces, slots, kv_heads, group, tokens, pages,
    place_ref, live_ref, key_scale_ref, value_scale_ref, *refs,
):
    query_refs = refs[:pieces]
    key_ref, value_ref, out_ref, queries, outs = refs[pieces:]
    heads = kv_heads * group
    page_tokens = tokens // pages
    held = query_refs[0].shape[0]
    for piece, query_ref in enumerate(query_refs):
        block = query_ref[...].astype(jnp.float32)
        for head in range(heads):
            queries[pl.ds(piece * held * heads + head, held, stride=heads), :] = block[
                :, head * LANES : (head + 1) * LANES
            ]
    together = 2 if kv_heads % 2 == 0 else 1
    each = min(slots, LANES // heads)
    rows = together * group
    lane = lane_index((heads, LANES))
    token = lane_index((heads, page_tokens))
    upper = lax.broadcasted_iota(jnp.int32, (rows, LANES), 0) < group
    zero = jnp.zeros((rows, LANES), jnp.bfloat16)
    logs = jnp.zeros((heads, LANES), jnp.float32)

    def joined(ref, slot, kv):
        if together == 1:
            return ref[slot, kv]
        return jnp.concatenate([ref[slot, kv], ref[slot, kv + 1]], axis=1)

    for batch in range(slots // each):
        dotted = []
        for index in range(each):
            slot = batch * each + index
            start = pl.multiple_of(place_ref[slot] * heads, 8)
            query = queries[pl.ds(start, heads), :].astype(jnp.bfloat16)
            for kv in range(0, kv_heads, together):
                own = query[kv * group : kv * group + rows]
                if together == 2:
                    own = jnp.concatenate(
                        [jnp.where(upper, own, zero), jnp.where(upper, zero, own)], axis=1
                    )
                dotted.append(
                    lax.dot_general(
                        own,
                        joined(key_ref, slot, kv),
                        (((1,), (1,)), ((), ())),
                        preferred_element_type=jnp.float32,
                    )
                )
        dotted = jnp.concatenate(dotted, axis=0)
        scores = []
        for page in range(pages):
            part = dotted[:, page * page_tokens : (page + 1) * page_tokens]
            part = part * key_scale_ref[batch, page]
            masked = []
            for index in range(each):
                own = part[index * heads : (index + 1) * heads]
                live = live_ref[batch * each + index] - page * page_tokens
                masked.append(jnp.where(token < live, own, LOW))
            scores.append(jnp.concatenate(masked, axis=0) if each > 1 else masked[0])
        peak = jnp.max(functools.reduce(jnp.maximum, scores), axis=1, keepdims=True)
        total, weights = None, []
        for page in range(pages):
            expon = jnp.exp(scores[page] - peak)
            total = expon if total is None else total + expon
            weights.append((expon * value_scale_ref[batch, page]).astype(jnp.bfloat16))
        total = jnp.sum(total, axis=1, keepdims=True)
        weights = jnp.concatenate(weights, axis=1)
        scale = 1.0 / total
        log = peak + jnp.log(total)
        for index in range(each):
            slot = batch * each + index
            for kv in range(0, kv_heads, together):
                first = index * heads + kv * group
                partial = jnp.dot(
                    weights[first : first + rows],
                    joined(value_ref, slot, kv),
                    preferred_element_type=jnp.float32,
                )
                if together == 2:
                    partial = jnp.concatenate(
                        [partial[:group, :LANES], partial[group:, LANES:]], axis=0
                    )
                at = slot * heads + kv * group
                outs[at : at + rows, :] = partial * scale[first : first + rows]
            logs = jnp.where(lane == slot, log[index * heads : (index + 1) * heads], logs)
    out_ref[: slots * heads, :] = outs[...].astype(jnp.bfloat16)
    store_stats(out_ref, slots * heads, logs, slots, heads)


def merge_slots_kernel(groups, slots, rows, heads, owner_ref, *refs):
    out_ref, sums = refs[groups:]
    lane = lane_index((heads, LANES))
    owner = jnp.full((8, LANES), -1, jnp.int32)
    for at in range(groups * slots):
        owner = jnp.where(lane[:8] == at, owner_ref[at], owner)
    owner = jnp.concatenate([owner] * (heads // 8), axis=0)
    logs = jnp.full((heads, LANES), LOW, jnp.float32)
    for index in range(groups):
        own = load_stats(refs[index], slots * heads, slots, heads)
        own = pltpu.roll(own, index * slots, 1) if index else own
        inside = (lane >= index * slots) & (lane < (index + 1) * slots)
        logs = jnp.where(inside, own, logs)
    tops = jnp.zeros((heads, LANES), jnp.float32)
    row_top = []
    for row in range(rows):
        top = jnp.max(jnp.where(owner == row, logs, LOW), axis=1, keepdims=True)
        tops = jnp.where(owner == row, top, tops)
        row_top.append(top)
    factor = jnp.exp(logs - tops)
    totals = jnp.ones((heads, LANES), jnp.float32)
    row_logs = jnp.full((heads, LANES), LOW, jnp.float32)
    for row in range(rows):
        total = jnp.sum(jnp.where(owner == row, factor, 0.0), axis=1, keepdims=True)
        totals = jnp.where(owner == row, total, totals)
        held = total > 0.0
        value = jnp.where(held, row_top[row] + jnp.log(jnp.where(held, total, 1.0)), LOW)
        row_logs = jnp.where(lane == row, value, row_logs)
    weight = factor / totals
    sums[...] = jnp.zeros_like(sums)
    for index in range(groups):
        for slot in range(slots):
            at = index * slots + slot
            start = pl.multiple_of(owner_ref[at] * heads, 8)
            block = pl.ds(start, heads)
            sums[block, :] += weight[:, at : at + 1] * load_entry(refs[index], slot, heads)
    out_ref[: rows * heads, :] = sums[...].astype(jnp.bfloat16)
    store_stats(out_ref, rows * heads, row_logs, rows, heads)


def merge_rows(refs, rows, heads, sums):
    logs = [load_stats(ref, rows * heads, rows, heads) for ref in refs]
    top = functools.reduce(jnp.maximum, logs)
    factors = [jnp.exp(log - top) for log in logs]
    total = functools.reduce(jnp.add, factors)
    weights = [factor / total for factor in factors]
    for row in range(rows):
        parts = [
            weight[:, row : row + 1] * load_entry(ref, row, heads)
            for weight, ref in zip(weights, refs)
        ]
        sums[row * heads : (row + 1) * heads, :] = functools.reduce(jnp.add, parts)
    return top + jnp.log(total)


def merge_rows_kernel(groups, rows, heads, *refs):
    out_ref, sums = refs[groups:]
    logs = merge_rows(refs[:groups], rows, heads, sums)
    out_ref[: rows * heads, :] = sums[...].astype(jnp.bfloat16)
    store_stats(out_ref, rows * heads, logs, rows, heads)


def project_kernel(groups, rows, heads, halves, *refs):
    weight_ref, *out_refs, sums = refs[groups:]
    merge_rows(refs[:groups], rows, heads, sums)
    attention = jnp.concatenate(
        [sums[pl.ds(head, rows, stride=heads), :].astype(jnp.bfloat16) for head in range(heads)],
        axis=1,
    )
    mixed = jnp.dot(attention, weight_ref[...], preferred_element_type=jnp.float32)
    if halves:
        first = lax.axis_index("head") == 0
        lower, upper = mixed[: rows // 2], mixed[rows // 2 :]
        out_refs[0][...] = jnp.where(first, lower, upper)
        out_refs[1][...] = jnp.where(first, upper, lower)
    else:
        out_refs[0][...] = mixed


def per_device(
    query,
    key_codes,
    value_codes,
    key_scale,
    value_scale,
    out_weight,
    range_counts,
    last_fill,
    slot_table,
    *,
    devices,
    head_devices,
):
    slots, kv_heads, tokens, head_dim = key_codes.shape
    pages = key_scale.shape[2]
    rows = range_counts.shape[0]
    all_slots = slot_table.shape[0]
    heads = query.shape[1] // head_dim
    group = heads // kv_heads
    own_rows = query.shape[0]
    columns = out_weight.shape[1]
    spread = exchange_rounds(devices, 2)
    rounds = exchange_rounds(devices, 4)

    near = [0] + rounds[0]
    tables = jnp.concatenate([range_counts, last_fill, slot_table])
    own_slots = jax.ShapeDtypeStruct((slots,), jnp.int32)
    place, live, owner = pl.pallas_call(
        functools.partial(
            locate_kernel, spread, near, slots, rows, all_slots, own_rows, tokens
        ),
        out_shape=[own_slots, own_slots, jax.ShapeDtypeStruct((len(near) * slots,), jnp.int32)],
        in_specs=[SMEM],
        out_specs=[SMEM] * 3,
        scratch_shapes=[
            pltpu.SMEM((all_slots,), jnp.int32),
            pltpu.SMEM((rows,), jnp.int32),
        ],
        cost_estimate=pl.CostEstimate(
            flops=LOCATE_FLOPS, bytes_accessed=4 * all_slots, transcendentals=0
        ),
        compiler_params=pltpu.CompilerParams(vmem_limit_bytes=MIB),
        name="locate",
    )(tables)

    batches = slots // min(slots, LANES // heads)
    scales = pl.pallas_call(
        functools.partial(columns_kernel, group, head_dim**-0.5),
        out_shape=[
            jax.ShapeDtypeStruct(
                (batches, pages, slots // batches * heads, LANES), jnp.float32
            )
        ]
        * 2,
        in_specs=[VMEM] * 2,
        out_specs=[VMEM] * 2,
        compiler_params=pltpu.CompilerParams(vmem_limit_bytes=2 * MIB),
        name="columns",
    )(key_scale, value_scale)

    held = [query]
    for turn, masks in enumerate(spread):
        block = jnp.concatenate(held, axis=0) if len(held) > 1 else held[0]
        if turn == 1:
            block, place, live, owner = lax.optimization_barrier((block, place, live, owner))
        elif turn > 1:
            block = lax.optimization_barrier(block)
        held = [block] + [partner(block, mask, devices) for mask in masks]

    payload = (slots + stat_blocks(slots)) * heads
    held = [
        pl.pallas_call(
            functools.partial(
                attend_kernel, len(held), slots, kv_heads, group, tokens, pages
            ),
            out_shape=jax.ShapeDtypeStruct((payload, LANES), jnp.bfloat16),
            in_specs=[SMEM] * 2 + [VMEM] * (len(held) + 4),
            out_specs=VMEM,
            scratch_shapes=[
                pltpu.VMEM((rows * heads, LANES), jnp.float32),
                pltpu.VMEM((slots * heads, LANES), jnp.float32),
            ],
            compiler_params=pltpu.CompilerParams(vmem_limit_bytes=8 * MIB),
            cost_estimate=pl.CostEstimate(
                flops=ATTEND_FLOPS,
                bytes_accessed=4 * slots * kv_heads * tokens * head_dim,
                transcendentals=slots * heads * tokens,
            ),
            name="attend",
        )(
            place,
            live,
            *scales,
            *held,
            key_codes,
            value_codes,
        )
    ]

    payload = (rows + stat_blocks(rows)) * heads
    sums = pltpu.VMEM((rows * heads, LANES), jnp.float32)
    for turn, masks in enumerate(rounds):
        held = held + [partner(held[0], mask, devices) for mask in masks]
        groups = len(held)
        params = pltpu.CompilerParams(vmem_limit_bytes=8 * MIB)
        if turn == 0:
            held = [
                pl.pallas_call(
                    functools.partial(merge_slots_kernel, groups, slots, rows, heads),
                    out_shape=jax.ShapeDtypeStruct((payload, LANES), jnp.bfloat16),
                    in_specs=[SMEM] + [VMEM] * groups,
                    out_specs=VMEM,
                    scratch_shapes=[sums],
                    compiler_params=params,
                    cost_estimate=pl.CostEstimate(
                        flops=MERGE_FLOPS, bytes_accessed=2 * payload * LANES, transcendentals=0
                    ),
                    name="merge_slots",
                )(owner, *held)
            ]
        elif turn < len(rounds) - 1:
            held = [
                pl.pallas_call(
                    functools.partial(merge_rows_kernel, groups, rows, heads),
                    out_shape=jax.ShapeDtypeStruct((payload, LANES), jnp.bfloat16),
                    in_specs=[VMEM] * groups,
                    out_specs=VMEM,
                    scratch_shapes=[sums],
                    compiler_params=params,
                    name="merge_rows",
                )(*held)
            ]
    halves = head_devices == 2
    mixed_shape = jax.ShapeDtypeStruct((rows // (1 + halves), columns), jnp.float32)
    mixed, *give = pl.pallas_call(
        functools.partial(project_kernel, len(held), rows, heads, halves),
        out_shape=[mixed_shape] * (1 + halves),
        in_specs=[VMEM] * (len(held) + 1),
        out_specs=[VMEM] * (1 + halves),
        scratch_shapes=[sums],
        compiler_params=pltpu.CompilerParams(vmem_limit_bytes=8 * MIB),
        name="project",
    )(*held, out_weight)
    if halves:
        mixed = mixed + lax.ppermute(give[0], "head", [(0, 1), (1, 0)])
    else:
        mixed = lax.psum_scatter(mixed, "head", scatter_dimension=0, tiled=True)
    return mixed.astype(jnp.bfloat16)


def solution(mesh):
    return jax.shard_map(
        functools.partial(
            per_device, devices=mesh.shape["page"], head_devices=mesh.shape["head"]
        ),
        mesh=mesh,
        in_specs=(
            P("page", "head"),
            P("page", "head", None, None),
            P("page", "head", None, None),
            P("page", "head", None),
            P("page", "head", None),
            P("head", "page"),
            P(),
            P(),
            P(),
        ),
        out_specs=P("head", "page"),
        check_vma=False,
    )
```

```python
import functools

import jax
import jax.numpy as jnp
from jax import lax
from jax.experimental import pallas as pl
from jax.experimental.pallas import tpu as pltpu
from jax.sharding import PartitionSpec as P

LANES = 128
LOW = -1e30
LOCATE_FLOPS = 20_000_000_000
ATTEND_FLOPS = 5_000_000_000
MERGE_FLOPS = 20_000_000_000
MIB = 1 << 20
VMEM = pl.BlockSpec(memory_space=pltpu.VMEM)
SMEM = pl.BlockSpec(memory_space=pltpu.SMEM)


def exchange_masks(bits):
    masks = [0]
    for bit in bits:
        masks += [mask + bit for mask in masks]
    return masks[1:]


def spread_rounds(devices):
    bits = [1 << k for k in range(devices.bit_length() - 1)]
    return [[bit] for bit in reversed(bits[2:])] + [bits[:2]]


def merge_rounds(devices):
    bits = [1 << k for k in range(devices.bit_length() - 1)]
    pairs = [[bits[k], bits[-1 - k]] for k in range(len(bits) // 2)]
    return pairs + ([[bits[len(bits) // 2]]] if len(bits) % 2 else [])


def partner(value, mask, devices):
    return lax.ppermute(value, "page", [(i, i ^ mask) for i in range(devices)])


def stat_place(piece, entries):
    each = LANES // entries
    return piece // each, (piece % each) * entries


def stat_blocks(entries):
    return stat_place(2, entries)[0] + 1


def lane_index(shape):
    return lax.broadcasted_iota(jnp.int32, shape, 1)


def store_stats(out_ref, base, logs, entries, heads):
    high = logs.astype(jnp.bfloat16).astype(jnp.float32)
    middle = (logs - high).astype(jnp.bfloat16).astype(jnp.float32)
    low = logs - high - middle
    lane = lane_index((heads, LANES))
    blocks = [jnp.zeros((heads, LANES), jnp.float32) for _ in range(stat_blocks(entries))]
    for piece, value in enumerate((high, middle, low)):
        block, offset = stat_place(piece, entries)
        moved = pltpu.roll(value, offset, 1) if offset else value
        inside = (lane >= offset) & (lane < offset + entries)
        blocks[block] = jnp.where(inside, moved, blocks[block])
    table = jnp.concatenate(blocks, axis=0) if len(blocks) > 1 else blocks[0]
    out_ref[base : base + table.shape[0], :] = table.astype(jnp.bfloat16)


def load_stats(ref, base, entries, heads):
    rows = stat_blocks(entries) * heads
    table = ref[base : base + rows, :].astype(jnp.float32)
    total = None
    for piece in range(3):
        block, offset = stat_place(piece, entries)
        value = table[block * heads : (block + 1) * heads]
        value = pltpu.roll(value, LANES - offset, 1) if offset else value
        total = value if total is None else total + value
    return total


def load_entry(ref, index, heads):
    if heads % 16 == 0:
        return ref[index * heads : (index + 1) * heads, :].astype(jnp.float32)
    base = index * heads // 16 * 16
    block = ref[base : base + 16, :].astype(jnp.float32)
    return block[index * heads - base : (index + 1) * heads - base]


def locate_kernel(
    bits, near, slots, rows, all_slots, own_rows, tokens,
    table_ref, place_ref, live_ref, owner_ref, position_of, first_of,
):
    me = lax.axis_index("page")
    fills, entries = rows, 2 * rows

    def note(position, carry):
        position_of[table_ref[entries + position]] = position
        return carry

    lax.fori_loop(0, all_slots, note, 0, unroll=16)
    ends, end = [], jnp.int32(0)
    for row in range(rows):
        first_of[row] = end
        end = end + table_ref[row]
        ends.append(end)
    for index, mask in enumerate(near):
        source = jnp.bitwise_xor(me, mask)
        for slot in range(slots):
            position = position_of[source * slots + slot]
            row = functools.reduce(
                jnp.add, [(position >= end).astype(jnp.int32) for end in ends[:-1]]
            )
            owner_ref[index * slots + slot] = row
            if index == 0:
                away = jnp.bitwise_xor(row // own_rows, me)
                place, step_size = row % own_rows, own_rows
                for bit in bits:
                    place += away // bit % 2 * step_size
                    step_size *= 2
                place_ref[slot] = place
                before = position - first_of[row]
                live_ref[slot] = (table_ref[row] - 1 - before) * tokens + table_ref[fills + row]


def columns_kernel(group, factor, *refs):
    for scale_ref, out_ref, multiplier in zip(refs[:2], refs[2:], (factor, 1.0)):
        slots, kv_heads, pages = scale_ref.shape
        batches = out_ref.shape[0]
        each = slots // batches
        for batch in range(batches):
            parts = []
            for index in range(each):
                scale = scale_ref[batch * each + index] * multiplier
                for kv in range(kv_heads):
                    parts.append(jnp.broadcast_to(scale[kv : kv + 1], (group, pages)))
            table = jnp.concatenate(parts, axis=0)
            for page in range(pages):
                out_ref[batch, page] = jnp.broadcast_to(
                    table[:, page : page + 1], (table.shape[0], LANES)
                )


def attend_kernel(
    pieces, slots, kv_heads, group, tokens, pages,
    place_ref, live_ref, key_scale_ref, value_scale_ref, *refs,
):
    query_refs = refs[:pieces]
    key_ref, value_ref, out_ref, queries, outs = refs[pieces:]
    heads = kv_heads * group
    page_tokens = tokens // pages
    held = query_refs[0].shape[0]
    for piece, query_ref in enumerate(query_refs):
        block = query_ref[...].astype(jnp.float32)
        for head in range(heads):
            queries[pl.ds(piece * held * heads + head, held, stride=heads), :] = block[
                :, head * LANES : (head + 1) * LANES
            ]
    together = 2 if kv_heads % 2 == 0 else 1
    each = slots // key_scale_ref.shape[0]
    rows = together * group
    lane = lane_index((heads, LANES))
    token = lane_index((heads, page_tokens))
    upper = lax.broadcasted_iota(jnp.int32, (rows, LANES), 0) < group
    zero = jnp.zeros((rows, LANES), jnp.bfloat16)
    logs = jnp.zeros((heads, LANES), jnp.float32)

    def joined(ref, slot, kv):
        if together == 1:
            return ref[slot, kv]
        return jnp.concatenate([ref[slot, kv], ref[slot, kv + 1]], axis=1)

    def products(batch):
        dotted = []
        for index in range(each):
            slot = batch * each + index
            start = pl.multiple_of(place_ref[slot] * heads, 8)
            query = queries[pl.ds(start, heads), :].astype(jnp.bfloat16)
            for kv in range(0, kv_heads, together):
                own = query[kv * group : kv * group + rows]
                if together == 2:
                    own = jnp.concatenate(
                        [jnp.where(upper, own, zero), jnp.where(upper, zero, own)], axis=1
                    )
                dotted.append(
                    lax.dot_general(
                        own,
                        joined(key_ref, slot, kv),
                        (((1,), (1,)), ((), ())),
                        preferred_element_type=jnp.float32,
                    )
                )
        return jnp.concatenate(dotted, axis=0)

    def softmax(batch, dotted):
        scores = []
        for page in range(pages):
            part = dotted[:, page * page_tokens : (page + 1) * page_tokens]
            part = part * key_scale_ref[batch, page]
            masked = []
            for index in range(each):
                own = part[index * heads : (index + 1) * heads]
                live = live_ref[batch * each + index] - page * page_tokens
                masked.append(jnp.where(token < live, own, LOW))
            scores.append(jnp.concatenate(masked, axis=0) if each > 1 else masked[0])
        peak = jnp.max(functools.reduce(jnp.maximum, scores), axis=1, keepdims=True)
        total, weights = None, []
        for page in range(pages):
            expon = jnp.exp(scores[page] - peak)
            total = expon if total is None else total + expon
            weights.append((expon * value_scale_ref[batch, page]).astype(jnp.bfloat16))
        total = jnp.sum(total, axis=1, keepdims=True)
        return jnp.concatenate(weights, axis=1), 1.0 / total, peak + jnp.log(total)

    def sums(batch, weights, scale):
        for index in range(each):
            slot = batch * each + index
            for kv in range(0, kv_heads, together):
                first = index * heads + kv * group
                partial = jnp.dot(
                    weights[first : first + rows],
                    joined(value_ref, slot, kv),
                    preferred_element_type=jnp.float32,
                )
                if together == 2:
                    partial = jnp.concatenate(
                        [partial[:group, :LANES], partial[group:, LANES:]], axis=0
                    )
                at = slot * heads + kv * group
                outs[at : at + rows, :] = partial * scale[first : first + rows]

    batches = key_scale_ref.shape[0]
    ready = products(0)
    for batch in range(batches):
        following = products(batch + 1) if batch + 1 < batches else None
        weights, scale, log = softmax(batch, ready)
        sums(batch, weights, scale)
        ready = following
        for index in range(each):
            slot = batch * each + index
            logs = jnp.where(lane == slot, log[index * heads : (index + 1) * heads], logs)

    out_ref[: slots * heads, :] = outs[...].astype(jnp.bfloat16)
    store_stats(out_ref, slots * heads, logs, slots, heads)


def merge_slots_kernel(groups, slots, rows, heads, owner_ref, *refs):
    out_ref, sums = refs[groups:]
    lane = lane_index((heads, LANES))
    owner = jnp.full((8, LANES), -1, jnp.int32)
    for at in range(groups * slots):
        owner = jnp.where(lane[:8] == at, owner_ref[at], owner)
    owner = jnp.concatenate([owner] * (heads // 8), axis=0)
    logs = jnp.full((heads, LANES), LOW, jnp.float32)
    for index in range(groups):
        own = load_stats(refs[index], slots * heads, slots, heads)
        own = pltpu.roll(own, index * slots, 1) if index else own
        inside = (lane >= index * slots) & (lane < (index + 1) * slots)
        logs = jnp.where(inside, own, logs)
    tops = jnp.zeros((heads, LANES), jnp.float32)
    row_top = []
    for row in range(rows):
        top = jnp.max(jnp.where(owner == row, logs, LOW), axis=1, keepdims=True)
        tops = jnp.where(owner == row, top, tops)
        row_top.append(top)
    factor = jnp.exp(logs - tops)
    totals = jnp.ones((heads, LANES), jnp.float32)
    row_logs = jnp.full((heads, LANES), LOW, jnp.float32)
    for row in range(rows):
        total = jnp.sum(jnp.where(owner == row, factor, 0.0), axis=1, keepdims=True)
        totals = jnp.where(owner == row, total, totals)
        held = total > 0.0
        value = jnp.where(held, row_top[row] + jnp.log(jnp.where(held, total, 1.0)), LOW)
        row_logs = jnp.where(lane == row, value, row_logs)
    weight = factor / totals
    sums[...] = jnp.zeros_like(sums)
    for index in range(groups):
        for slot in range(slots):
            at = index * slots + slot
            start = pl.multiple_of(owner_ref[at] * heads, 8)
            block = pl.ds(start, heads)
            sums[block, :] += weight[:, at : at + 1] * load_entry(refs[index], slot, heads)
    out_ref[: rows * heads, :] = sums[...].astype(jnp.bfloat16)
    store_stats(out_ref, rows * heads, row_logs, rows, heads)


def merge_rows(refs, rows, heads, sums):
    logs = [load_stats(ref, rows * heads, rows, heads) for ref in refs]
    top = functools.reduce(jnp.maximum, logs)
    factors = [jnp.exp(log - top) for log in logs]
    total = functools.reduce(jnp.add, factors)
    weights = [factor / total for factor in factors]
    for row in range(rows):
        parts = [
            weight[:, row : row + 1] * load_entry(ref, row, heads)
            for weight, ref in zip(weights, refs)
        ]
        sums[row * heads : (row + 1) * heads, :] = functools.reduce(jnp.add, parts)
    return top + jnp.log(total)


def merge_rows_kernel(groups, rows, heads, *refs):
    out_ref, sums = refs[groups:]
    logs = merge_rows(refs[:groups], rows, heads, sums)
    out_ref[: rows * heads, :] = sums[...].astype(jnp.bfloat16)
    store_stats(out_ref, rows * heads, logs, rows, heads)


def project_kernel(groups, rows, heads, halves, *refs):
    weight_ref, *out_refs, sums = refs[groups:]
    merge_rows(refs[:groups], rows, heads, sums)
    attention = jnp.concatenate(
        [sums[pl.ds(head, rows, stride=heads), :].astype(jnp.bfloat16) for head in range(heads)],
        axis=1,
    )
    mixed = jnp.dot(attention, weight_ref[...], preferred_element_type=jnp.float32)
    if halves:
        first = lax.axis_index("head") == 0
        lower, upper = mixed[: rows // 2], mixed[rows // 2 :]
        out_refs[0][...] = jnp.where(first, lower, upper)
        out_refs[1][...] = jnp.where(first, upper, lower)
    else:
        out_refs[0][...] = mixed


def per_device(
    query,
    key_codes,
    value_codes,
    key_scale,
    value_scale,
    out_weight,
    range_counts,
    last_fill,
    slot_table,
    *,
    devices,
    head_devices,
):
    slots, kv_heads, tokens, head_dim = key_codes.shape
    pages = key_scale.shape[2]
    rows = range_counts.shape[0]
    all_slots = slot_table.shape[0]
    heads = query.shape[1] // head_dim
    group = heads // kv_heads
    own_rows = query.shape[0]
    columns = out_weight.shape[1]
    spread = spread_rounds(devices)
    rounds = [exchange_masks(bits) for bits in merge_rounds(devices)]

    near = [0] + rounds[0]
    tables = jnp.concatenate([range_counts, last_fill, slot_table])
    own_slots = jax.ShapeDtypeStruct((slots,), jnp.int32)
    place, live, owner = pl.pallas_call(
        functools.partial(
            locate_kernel, sum(spread, []), near, slots, rows, all_slots, own_rows, tokens
        ),
        out_shape=[own_slots, own_slots, jax.ShapeDtypeStruct((len(near) * slots,), jnp.int32)],
        in_specs=[SMEM],
        out_specs=[SMEM] * 3,
        scratch_shapes=[
            pltpu.SMEM((all_slots,), jnp.int32),
            pltpu.SMEM((rows,), jnp.int32),
        ],
        cost_estimate=pl.CostEstimate(
            flops=LOCATE_FLOPS, bytes_accessed=4 * all_slots, transcendentals=0
        ),
        compiler_params=pltpu.CompilerParams(vmem_limit_bytes=MIB),
        name="locate",
    )(tables)

    batches = slots // 2 if slots % 2 == 0 else slots
    scales = pl.pallas_call(
        functools.partial(columns_kernel, group, head_dim**-0.5),
        out_shape=[
            jax.ShapeDtypeStruct(
                (batches, pages, slots // batches * heads, LANES), jnp.float32
            )
        ]
        * 2,
        in_specs=[VMEM] * 2,
        out_specs=[VMEM] * 2,
        compiler_params=pltpu.CompilerParams(vmem_limit_bytes=2 * MIB),
        name="columns",
    )(key_scale, value_scale)

    held = [query]
    for turn, bits in enumerate(spread):
        block = jnp.concatenate(held, axis=0) if len(held) > 1 else held[0]
        if turn == 1:
            block, place, live, owner = lax.optimization_barrier((block, place, live, owner))
        elif turn > 1:
            block = lax.optimization_barrier(block)
        held = [block] + [partner(block, mask, devices) for mask in exchange_masks(bits)]

    payload = (slots + stat_blocks(slots)) * heads
    held = [
        pl.pallas_call(
            functools.partial(
                attend_kernel, len(held), slots, kv_heads, group, tokens, pages
            ),
            out_shape=jax.ShapeDtypeStruct((payload, LANES), jnp.bfloat16),
            in_specs=[SMEM] * 2 + [VMEM] * (len(held) + 4),
            out_specs=VMEM,
            scratch_shapes=[
                pltpu.VMEM((rows * heads, LANES), jnp.float32),
                pltpu.VMEM((slots * heads, LANES), jnp.float32),
            ],
            compiler_params=pltpu.CompilerParams(vmem_limit_bytes=8 * MIB),
            cost_estimate=pl.CostEstimate(
                flops=ATTEND_FLOPS,
                bytes_accessed=4 * slots * kv_heads * tokens * head_dim,
                transcendentals=slots * heads * tokens,
            ),
            name="attend",
        )(
            place,
            live,
            *scales,
            *held,
            key_codes,
            value_codes,
        )
    ]

    payload = (rows + stat_blocks(rows)) * heads
    sums = pltpu.VMEM((rows * heads, LANES), jnp.float32)
    for turn, masks in enumerate(rounds):
        held = held + [partner(held[0], mask, devices) for mask in masks]
        groups = len(held)
        params = pltpu.CompilerParams(vmem_limit_bytes=8 * MIB)
        if turn == 0:
            held = [
                pl.pallas_call(
                    functools.partial(merge_slots_kernel, groups, slots, rows, heads),
                    out_shape=jax.ShapeDtypeStruct((payload, LANES), jnp.bfloat16),
                    in_specs=[SMEM] + [VMEM] * groups,
                    out_specs=VMEM,
                    scratch_shapes=[sums],
                    compiler_params=params,
                    cost_estimate=pl.CostEstimate(
                        flops=MERGE_FLOPS, bytes_accessed=2 * payload * LANES, transcendentals=0
                    ),
                    name="merge_slots",
                )(owner, *held)
            ]
        elif turn < len(rounds) - 1:
            held = [
                pl.pallas_call(
                    functools.partial(merge_rows_kernel, groups, rows, heads),
                    out_shape=jax.ShapeDtypeStruct((payload, LANES), jnp.bfloat16),
                    in_specs=[VMEM] * groups,
                    out_specs=VMEM,
                    scratch_shapes=[sums],
                    compiler_params=params,
                    name="merge_rows",
                )(*held)
            ]
    halves = head_devices == 2
    mixed_shape = jax.ShapeDtypeStruct((rows // (1 + halves), columns), jnp.float32)
    mixed, *give = pl.pallas_call(
        functools.partial(project_kernel, len(held), rows, heads, halves),
        out_shape=[mixed_shape] * (1 + halves),
        in_specs=[VMEM] * (len(held) + 1),
        out_specs=[VMEM] * (1 + halves),
        scratch_shapes=[sums],
        compiler_params=pltpu.CompilerParams(vmem_limit_bytes=8 * MIB),
        name="project",
    )(*held, out_weight)
    if halves:
        mixed = mixed + lax.ppermute(give[0], "head", [(0, 1), (1, 0)])
    else:
        mixed = lax.psum_scatter(mixed, "head", scatter_dimension=0, tiled=True)
    return mixed.astype(jnp.bfloat16)


def solution(mesh):
    return jax.shard_map(
        functools.partial(
            per_device, devices=mesh.shape["page"], head_devices=mesh.shape["head"]
        ),
        mesh=mesh,
        in_specs=(
            P("page", "head"),
            P("page", "head", None, None),
            P("page", "head", None, None),
            P("page", "head", None),
            P("page", "head", None),
            P("head", "page"),
            P(),
            P(),
            P(),
        ),
        out_specs=P("head", "page"),
        check_vma=False,
    )
```

```python
import functools

import jax
import jax.numpy as jnp
from jax import lax
from jax.experimental import pallas as pl
from jax.experimental.pallas import tpu as pltpu
from jax.sharding import PartitionSpec as P

LANES = 128
LOW = -1e30
LOCATE_FLOPS = 20_000_000_000
ATTEND_FLOPS = 5_000_000_000
MERGE_FLOPS = 20_000_000_000
MIB = 1 << 20
VMEM = pl.BlockSpec(memory_space=pltpu.VMEM)
SMEM = pl.BlockSpec(memory_space=pltpu.SMEM)


def exchange_masks(bits):
    masks = [0]
    for bit in bits:
        masks += [mask + bit for mask in masks]
    return masks[1:]


def spread_rounds(devices):
    bits = [1 << k for k in range(devices.bit_length() - 1)]
    return [[bit] for bit in reversed(bits[2:])] + [bits[:2]]


def merge_rounds(devices):
    bits = [1 << k for k in range(devices.bit_length() - 1)]
    pairs = [[bits[k], bits[-1 - k]] for k in range(len(bits) // 2)]
    return pairs + ([[bits[len(bits) // 2]]] if len(bits) % 2 else [])


def partner(value, mask, devices):
    return lax.ppermute(value, "page", [(i, i ^ mask) for i in range(devices)])


def stat_place(piece, entries):
    each = LANES // entries
    return piece // each, (piece % each) * entries


def stat_blocks(entries):
    return stat_place(2, entries)[0] + 1


def lane_index(shape):
    return lax.broadcasted_iota(jnp.int32, shape, 1)


def store_stats(out_ref, base, logs, entries, heads):
    high = logs.astype(jnp.bfloat16).astype(jnp.float32)
    middle = (logs - high).astype(jnp.bfloat16).astype(jnp.float32)
    low = logs - high - middle
    lane = lane_index((heads, LANES))
    blocks = [jnp.zeros((heads, LANES), jnp.float32) for _ in range(stat_blocks(entries))]
    for piece, value in enumerate((high, middle, low)):
        block, offset = stat_place(piece, entries)
        moved = pltpu.roll(value, offset, 1) if offset else value
        inside = (lane >= offset) & (lane < offset + entries)
        blocks[block] = jnp.where(inside, moved, blocks[block])
    table = jnp.concatenate(blocks, axis=0) if len(blocks) > 1 else blocks[0]
    out_ref[base : base + table.shape[0], :] = table.astype(jnp.bfloat16)


def load_stats(ref, base, entries, heads):
    rows = stat_blocks(entries) * heads
    table = ref[base : base + rows, :].astype(jnp.float32)
    total = None
    for piece in range(3):
        block, offset = stat_place(piece, entries)
        value = table[block * heads : (block + 1) * heads]
        value = pltpu.roll(value, LANES - offset, 1) if offset else value
        total = value if total is None else total + value
    return total


def load_entry(ref, index, heads):
    if heads % 16 == 0:
        return ref[index * heads : (index + 1) * heads, :].astype(jnp.float32)
    base = index * heads // 16 * 16
    block = ref[base : base + 16, :].astype(jnp.float32)
    return block[index * heads - base : (index + 1) * heads - base]


def locate_kernel(
    bits, near, slots, rows, all_slots, own_rows, tokens,
    table_ref, out_ref, position_of, first_of,
):
    me = lax.axis_index("page")
    fills, entries = rows, 2 * rows
    lane = lane_index((1, LANES))
    places = jnp.zeros((1, LANES), jnp.int32)
    lives = jnp.zeros((1, LANES), jnp.int32)
    owners = jnp.full((1, LANES), -1, jnp.int32)

    def note(position, carry):
        position_of[table_ref[entries + position]] = position
        return carry

    lax.fori_loop(0, all_slots, note, 0, unroll=16)
    ends, end = [], jnp.int32(0)
    for row in range(rows):
        first_of[row] = end
        end = end + table_ref[row]
        ends.append(end)
    for index, mask in enumerate(near):
        source = jnp.bitwise_xor(me, mask)
        for slot in range(slots):
            position = position_of[source * slots + slot]
            row = functools.reduce(
                jnp.add, [(position >= end).astype(jnp.int32) for end in ends[:-1]]
            )
            owners = jnp.where(lane == index * slots + slot, row, owners)
            if index == 0:
                away = jnp.bitwise_xor(row // own_rows, me)
                place, step_size = row % own_rows, own_rows
                for bit in bits:
                    place += away // bit % 2 * step_size
                    step_size *= 2
                places = jnp.where(lane == slot, place, places)
                before = position - first_of[row]
                live = (table_ref[row] - 1 - before) * tokens + table_ref[fills + row]
                lives = jnp.where(lane == slot, live, lives)
    out_ref[...] = jnp.concatenate(
        [places, lives, owners, jnp.zeros((5, LANES), jnp.int32)], axis=0
    )


def columns_kernel(group, factor, *refs):
    for scale_ref, out_ref, multiplier in zip(refs[:2], refs[2:], (factor, 1.0)):
        slots, kv_heads, pages = scale_ref.shape
        batches = out_ref.shape[0]
        each = slots // batches
        for batch in range(batches):
            parts = []
            for index in range(each):
                scale = scale_ref[batch * each + index] * multiplier
                for kv in range(kv_heads):
                    parts.append(jnp.broadcast_to(scale[kv : kv + 1], (group, pages)))
            table = jnp.concatenate(parts, axis=0)
            for page in range(pages):
                out_ref[batch, page] = jnp.broadcast_to(
                    table[:, page : page + 1], (table.shape[0], LANES)
                )


def attend_kernel(
    pieces, slots, kv_heads, group, tokens, pages,
    located_ref, key_scale_ref, value_scale_ref, *refs,
):
    query_refs = refs[:pieces]
    key_ref, value_ref, out_ref, queries, outs = refs[pieces:]
    heads = kv_heads * group
    page_tokens = tokens // pages
    held = query_refs[0].shape[0]
    for piece, query_ref in enumerate(query_refs):
        block = query_ref[...].astype(jnp.float32)
        for head in range(heads):
            queries[pl.ds(piece * held * heads + head, held, stride=heads), :] = block[
                :, head * LANES : (head + 1) * LANES
            ]
    together = 2 if kv_heads % 2 == 0 else 1
    each = slots // key_scale_ref.shape[0]
    rows = together * group
    lane = lane_index((heads, LANES))
    token = lane_index((heads, page_tokens))
    upper = lax.broadcasted_iota(jnp.int32, (rows, LANES), 0) < group
    zero = jnp.zeros((rows, LANES), jnp.bfloat16)
    logs = jnp.zeros((heads, LANES), jnp.float32)

    lives = [
        jnp.broadcast_to(located_ref[1:2, slot : slot + 1], (heads, page_tokens))
        for slot in range(slots)
    ]

    def joined(ref, slot, kv):
        if together == 1:
            return ref[slot, kv]
        return jnp.concatenate([ref[slot, kv], ref[slot, kv + 1]], axis=1)

    def products(batch):
        dotted = []
        for index in range(each):
            slot = batch * each + index
            start = pl.multiple_of(located_ref[0, slot] * heads, 8)
            query = queries[pl.ds(start, heads), :].astype(jnp.bfloat16)
            for kv in range(0, kv_heads, together):
                own = query[kv * group : kv * group + rows]
                if together == 2:
                    own = jnp.concatenate(
                        [jnp.where(upper, own, zero), jnp.where(upper, zero, own)], axis=1
                    )
                dotted.append(
                    lax.dot_general(
                        own,
                        joined(key_ref, slot, kv),
                        (((1,), (1,)), ((), ())),
                        preferred_element_type=jnp.float32,
                    )
                )
        return jnp.concatenate(dotted, axis=0)

    def softmax(batch, dotted):
        scores = []
        for page in range(pages):
            part = dotted[:, page * page_tokens : (page + 1) * page_tokens]
            part = part * key_scale_ref[batch, page]
            masked = []
            for index in range(each):
                own = part[index * heads : (index + 1) * heads]
                live = lives[batch * each + index]
                masked.append(jnp.where(token + page * page_tokens < live, own, LOW))
            scores.append(jnp.concatenate(masked, axis=0) if each > 1 else masked[0])
        peak = jnp.max(functools.reduce(jnp.maximum, scores), axis=1, keepdims=True)
        total, weights = None, []
        for page in range(pages):
            expon = jnp.exp(scores[page] - peak)
            total = expon if total is None else total + expon
            weights.append((expon * value_scale_ref[batch, page]).astype(jnp.bfloat16))
        total = jnp.sum(total, axis=1, keepdims=True)
        return jnp.concatenate(weights, axis=1), 1.0 / total, peak + jnp.log(total)

    def sums(batch, weights, scale):
        for index in range(each):
            slot = batch * each + index
            for kv in range(0, kv_heads, together):
                first = index * heads + kv * group
                partial = jnp.dot(
                    weights[first : first + rows],
                    joined(value_ref, slot, kv),
                    preferred_element_type=jnp.float32,
                )
                if together == 2:
                    partial = jnp.concatenate(
                        [partial[:group, :LANES], partial[group:, LANES:]], axis=0
                    )
                at = slot * heads + kv * group
                outs[at : at + rows, :] = partial * scale[first : first + rows]

    batches = key_scale_ref.shape[0]
    ready = products(0)
    for batch in range(batches):
        following = products(batch + 1) if batch + 1 < batches else None
        weights, scale, log = softmax(batch, ready)
        sums(batch, weights, scale)
        ready = following
        for index in range(each):
            slot = batch * each + index
            logs = jnp.where(lane == slot, log[index * heads : (index + 1) * heads], logs)

    out_ref[: slots * heads, :] = outs[...].astype(jnp.bfloat16)
    store_stats(out_ref, slots * heads, logs, slots, heads)


def merge_slots_kernel(groups, slots, rows, heads, located_ref, *refs):
    out_ref, sums = refs[groups:]
    lane = lane_index((heads, LANES))
    owner = jnp.broadcast_to(located_ref[2:3, :], (heads, LANES))
    logs = jnp.full((heads, LANES), LOW, jnp.float32)
    for index in range(groups):
        own = load_stats(refs[index], slots * heads, slots, heads)
        own = pltpu.roll(own, index * slots, 1) if index else own
        inside = (lane >= index * slots) & (lane < (index + 1) * slots)
        logs = jnp.where(inside, own, logs)
    tops = jnp.zeros((heads, LANES), jnp.float32)
    row_top = []
    for row in range(rows):
        top = jnp.max(jnp.where(owner == row, logs, LOW), axis=1, keepdims=True)
        tops = jnp.where(owner == row, top, tops)
        row_top.append(top)
    factor = jnp.exp(logs - tops)
    totals = jnp.ones((heads, LANES), jnp.float32)
    row_logs = jnp.full((heads, LANES), LOW, jnp.float32)
    for row in range(rows):
        total = jnp.sum(jnp.where(owner == row, factor, 0.0), axis=1, keepdims=True)
        totals = jnp.where(owner == row, total, totals)
        held = total > 0.0
        value = jnp.where(held, row_top[row] + jnp.log(jnp.where(held, total, 1.0)), LOW)
        row_logs = jnp.where(lane == row, value, row_logs)
    weight = factor / totals
    sums[...] = jnp.zeros_like(sums)
    for index in range(groups):
        for slot in range(slots):
            at = index * slots + slot
            start = pl.multiple_of(located_ref[2, at] * heads, 8)
            block = pl.ds(start, heads)
            sums[block, :] += weight[:, at : at + 1] * load_entry(refs[index], slot, heads)
    out_ref[: rows * heads, :] = sums[...].astype(jnp.bfloat16)
    store_stats(out_ref, rows * heads, row_logs, rows, heads)


def merge_rows(refs, rows, heads, sums):
    logs = [load_stats(ref, rows * heads, rows, heads) for ref in refs]
    top = functools.reduce(jnp.maximum, logs)
    factors = [jnp.exp(log - top) for log in logs]
    total = functools.reduce(jnp.add, factors)
    weights = [factor / total for factor in factors]
    for row in range(rows):
        parts = [
            weight[:, row : row + 1] * load_entry(ref, row, heads)
            for weight, ref in zip(weights, refs)
        ]
        sums[row * heads : (row + 1) * heads, :] = functools.reduce(jnp.add, parts)
    return top + jnp.log(total)


def merge_rows_kernel(groups, rows, heads, *refs):
    out_ref, sums = refs[groups:]
    logs = merge_rows(refs[:groups], rows, heads, sums)
    out_ref[: rows * heads, :] = sums[...].astype(jnp.bfloat16)
    store_stats(out_ref, rows * heads, logs, rows, heads)


def project_kernel(groups, rows, heads, halves, *refs):
    weight_ref, *out_refs, sums = refs[groups:]
    merge_rows(refs[:groups], rows, heads, sums)
    attention = jnp.concatenate(
        [sums[pl.ds(head, rows, stride=heads), :].astype(jnp.bfloat16) for head in range(heads)],
        axis=1,
    )
    mixed = jnp.dot(attention, weight_ref[...], preferred_element_type=jnp.float32)
    if halves:
        first = lax.axis_index("head") == 0
        lower, upper = mixed[: rows // 2], mixed[rows // 2 :]
        out_refs[0][...] = jnp.where(first, lower, upper)
        out_refs[1][...] = jnp.where(first, upper, lower)
    else:
        out_refs[0][...] = mixed


def per_device(
    query,
    key_codes,
    value_codes,
    key_scale,
    value_scale,
    out_weight,
    range_counts,
    last_fill,
    slot_table,
    *,
    devices,
    head_devices,
):
    slots, kv_heads, tokens, head_dim = key_codes.shape
    pages = key_scale.shape[2]
    rows = range_counts.shape[0]
    all_slots = slot_table.shape[0]
    heads = query.shape[1] // head_dim
    group = heads // kv_heads
    own_rows = query.shape[0]
    columns = out_weight.shape[1]
    spread = spread_rounds(devices)
    rounds = [exchange_masks(bits) for bits in merge_rounds(devices)]

    near = [0] + rounds[0]
    tables = jnp.concatenate([range_counts, last_fill, slot_table])
    located = pl.pallas_call(
        functools.partial(
            locate_kernel, sum(spread, []), near, slots, rows, all_slots, own_rows, tokens
        ),
        out_shape=jax.ShapeDtypeStruct((8, LANES), jnp.int32),
        in_specs=[SMEM],
        out_specs=VMEM,
        scratch_shapes=[
            pltpu.SMEM((all_slots,), jnp.int32),
            pltpu.SMEM((rows,), jnp.int32),
        ],
        cost_estimate=pl.CostEstimate(
            flops=LOCATE_FLOPS, bytes_accessed=4 * all_slots, transcendentals=0
        ),
        compiler_params=pltpu.CompilerParams(vmem_limit_bytes=MIB),
        name="locate",
    )(tables)

    batches = slots // 2 if slots % 2 == 0 else slots
    scales = pl.pallas_call(
        functools.partial(columns_kernel, group, head_dim**-0.5),
        out_shape=[
            jax.ShapeDtypeStruct(
                (batches, pages, slots // batches * heads, LANES), jnp.float32
            )
        ]
        * 2,
        in_specs=[VMEM] * 2,
        out_specs=[VMEM] * 2,
        compiler_params=pltpu.CompilerParams(vmem_limit_bytes=2 * MIB),
        name="columns",
    )(key_scale, value_scale)

    held = [query]
    for turn, bits in enumerate(spread):
        block = jnp.concatenate(held, axis=0) if len(held) > 1 else held[0]
        if turn == 1:
            block, located = lax.optimization_barrier((block, located))
        elif turn > 1:
            block = lax.optimization_barrier(block)
        held = [block] + [partner(block, mask, devices) for mask in exchange_masks(bits)]

    payload = (slots + stat_blocks(slots)) * heads
    held = [
        pl.pallas_call(
            functools.partial(
                attend_kernel, len(held), slots, kv_heads, group, tokens, pages
            ),
            out_shape=jax.ShapeDtypeStruct((payload, LANES), jnp.bfloat16),
            in_specs=[VMEM] * (len(held) + 5),
            out_specs=VMEM,
            scratch_shapes=[
                pltpu.VMEM((rows * heads, LANES), jnp.float32),
                pltpu.VMEM((slots * heads, LANES), jnp.float32),
            ],
            compiler_params=pltpu.CompilerParams(vmem_limit_bytes=8 * MIB),
            cost_estimate=pl.CostEstimate(
                flops=ATTEND_FLOPS,
                bytes_accessed=4 * slots * kv_heads * tokens * head_dim,
                transcendentals=slots * heads * tokens,
            ),
            name="attend",
        )(
            located,
            *scales,
            *held,
            key_codes,
            value_codes,
        )
    ]

    payload = (rows + stat_blocks(rows)) * heads
    sums = pltpu.VMEM((rows * heads, LANES), jnp.float32)
    for turn, masks in enumerate(rounds):
        held = held + [partner(held[0], mask, devices) for mask in masks]
        groups = len(held)
        params = pltpu.CompilerParams(vmem_limit_bytes=8 * MIB)
        if turn == 0:
            held = [
                pl.pallas_call(
                    functools.partial(merge_slots_kernel, groups, slots, rows, heads),
                    out_shape=jax.ShapeDtypeStruct((payload, LANES), jnp.bfloat16),
                    in_specs=[VMEM] * (groups + 1),
                    out_specs=VMEM,
                    scratch_shapes=[sums],
                    compiler_params=params,
                    cost_estimate=pl.CostEstimate(
                        flops=MERGE_FLOPS, bytes_accessed=2 * payload * LANES, transcendentals=0
                    ),
                    name="merge_slots",
                )(located, *held)
            ]
        elif turn < len(rounds) - 1:
            held = [
                pl.pallas_call(
                    functools.partial(merge_rows_kernel, groups, rows, heads),
                    out_shape=jax.ShapeDtypeStruct((payload, LANES), jnp.bfloat16),
                    in_specs=[VMEM] * groups,
                    out_specs=VMEM,
                    scratch_shapes=[sums],
                    compiler_params=params,
                    name="merge_rows",
                )(*held)
            ]
    halves = head_devices == 2
    mixed_shape = jax.ShapeDtypeStruct((rows // (1 + halves), columns), jnp.float32)
    mixed, *give = pl.pallas_call(
        functools.partial(project_kernel, len(held), rows, heads, halves),
        out_shape=[mixed_shape] * (1 + halves),
        in_specs=[VMEM] * (len(held) + 1),
        out_specs=[VMEM] * (1 + halves),
        scratch_shapes=[sums],
        compiler_params=pltpu.CompilerParams(vmem_limit_bytes=8 * MIB),
        name="project",
    )(*held, out_weight)
    if halves:
        mixed = mixed + lax.ppermute(give[0], "head", [(0, 1), (1, 0)])
    else:
        mixed = lax.psum_scatter(mixed, "head", scatter_dimension=0, tiled=True)
    return mixed.astype(jnp.bfloat16)


def solution(mesh):
    return jax.shard_map(
        functools.partial(
            per_device, devices=mesh.shape["page"], head_devices=mesh.shape["head"]
        ),
        mesh=mesh,
        in_specs=(
            P("page", "head"),
            P("page", "head", None, None),
            P("page", "head", None, None),
            P("page", "head", None),
            P("page", "head", None),
            P("head", "page"),
            P(),
            P(),
            P(),
        ),
        out_specs=P("head", "page"),
        check_vma=False,
    )
```

```python
import functools

import jax
import jax.numpy as jnp
from jax import lax
from jax.experimental import pallas as pl
from jax.experimental.pallas import tpu as pltpu
from jax.sharding import PartitionSpec as P

LANES = 128
LOW = -1e30
LOCATE_FLOPS = 20_000_000_000
ATTEND_FLOPS = 5_000_000_000
MERGE_FLOPS = 20_000_000_000
MIB = 1 << 20
VMEM = pl.BlockSpec(memory_space=pltpu.VMEM)
SMEM = pl.BlockSpec(memory_space=pltpu.SMEM)


def exchange_masks(bits):
    masks = [0]
    for bit in bits:
        masks += [mask + bit for mask in masks]
    return masks[1:]


def spread_rounds(devices):
    bits = [1 << k for k in range(devices.bit_length() - 1)]
    return [bits[:2]] + [bits[k : k + 2] for k in range(2, len(bits), 2)]


def merge_rounds(devices):
    bits = [1 << k for k in range(devices.bit_length() - 1)]
    pairs = [[bits[-1 - k], bits[k]] for k in range(len(bits) // 2)]
    pairs[0] = pairs[0][::-1]
    return pairs + ([[bits[len(bits) // 2]]] if len(bits) % 2 else [])


def partner(value, mask, devices):
    return lax.ppermute(value, "page", [(i, i ^ mask) for i in range(devices)])


def stat_place(piece, entries):
    each = LANES // entries
    return piece // each, (piece % each) * entries


def stat_blocks(entries):
    return stat_place(2, entries)[0] + 1


def lane_index(shape):
    return lax.broadcasted_iota(jnp.int32, shape, 1)


def store_stats(out_ref, base, logs, entries, heads):
    high = logs.astype(jnp.bfloat16).astype(jnp.float32)
    middle = (logs - high).astype(jnp.bfloat16).astype(jnp.float32)
    low = logs - high - middle
    lane = lane_index((heads, LANES))
    blocks = [jnp.zeros((heads, LANES), jnp.float32) for _ in range(stat_blocks(entries))]
    for piece, value in enumerate((high, middle, low)):
        block, offset = stat_place(piece, entries)
        moved = pltpu.roll(value, offset, 1) if offset else value
        inside = (lane >= offset) & (lane < offset + entries)
        blocks[block] = jnp.where(inside, moved, blocks[block])
    table = jnp.concatenate(blocks, axis=0) if len(blocks) > 1 else blocks[0]
    out_ref[base : base + table.shape[0], :] = table.astype(jnp.bfloat16)


def load_stats(ref, base, entries, heads):
    rows = stat_blocks(entries) * heads
    table = ref[base : base + rows, :].astype(jnp.float32)
    total = None
    for piece in range(3):
        block, offset = stat_place(piece, entries)
        value = table[block * heads : (block + 1) * heads]
        value = pltpu.roll(value, LANES - offset, 1) if offset else value
        total = value if total is None else total + value
    return total


def load_entry(ref, index, heads):
    if heads % 16 == 0:
        return ref[index * heads : (index + 1) * heads, :].astype(jnp.float32)
    base = index * heads // 16 * 16
    block = ref[base : base + 16, :].astype(jnp.float32)
    return block[index * heads - base : (index + 1) * heads - base]


def locate_kernel(
    bits, near, slots, rows, all_slots, own_rows, tokens,
    table_ref, out_ref, position_of, first_of,
):
    me = lax.axis_index("page")
    fills, entries = rows, 2 * rows
    lane = lane_index((1, LANES))
    places = jnp.zeros((1, LANES), jnp.int32)
    lives = jnp.zeros((1, LANES), jnp.int32)
    owners = jnp.full((1, LANES), -1, jnp.int32)

    def note(position, carry):
        position_of[table_ref[entries + position]] = position
        return carry

    lax.fori_loop(0, all_slots, note, 0, unroll=16)
    ends, end = [], jnp.int32(0)
    for row in range(rows):
        first_of[row] = end
        end = end + table_ref[row]
        ends.append(end)
    for index, mask in enumerate(near):
        source = jnp.bitwise_xor(me, mask)
        for slot in range(slots):
            position = position_of[source * slots + slot]
            row = functools.reduce(
                jnp.add, [(position >= end).astype(jnp.int32) for end in ends[:-1]]
            )
            owners = jnp.where(lane == index * slots + slot, row, owners)
            if index == 0:
                away = jnp.bitwise_xor(row // own_rows, me)
                place, step_size = row % own_rows, own_rows
                for bit in bits:
                    place += away // bit % 2 * step_size
                    step_size *= 2
                places = jnp.where(lane == slot, place, places)
                before = position - first_of[row]
                live = (table_ref[row] - 1 - before) * tokens + table_ref[fills + row]
                lives = jnp.where(lane == slot, live, lives)
    out_ref[...] = jnp.concatenate(
        [places, lives, owners, jnp.zeros((5, LANES), jnp.int32)], axis=0
    )


def columns_kernel(group, factor, *refs):
    for scale_ref, out_ref, multiplier in zip(refs[:2], refs[2:], (factor, 1.0)):
        slots, kv_heads, pages = scale_ref.shape
        batches = out_ref.shape[0]
        each = slots // batches
        for batch in range(batches):
            parts = []
            for index in range(each):
                scale = scale_ref[batch * each + index] * multiplier
                for kv in range(kv_heads):
                    parts.append(jnp.broadcast_to(scale[kv : kv + 1], (group, pages)))
            table = jnp.concatenate(parts, axis=0)
            for page in range(pages):
                out_ref[batch, page] = jnp.broadcast_to(
                    table[:, page : page + 1], (table.shape[0], LANES)
                )


def attend_kernel(
    pieces, slots, kv_heads, group, tokens, pages,
    located_ref, key_scale_ref, value_scale_ref, *refs,
):
    query_refs = refs[:pieces]
    key_ref, value_ref, out_ref, queries, outs = refs[pieces:]
    heads = kv_heads * group
    page_tokens = tokens // pages
    held = query_refs[0].shape[0]
    for piece, query_ref in enumerate(query_refs):
        block = query_ref[...].astype(jnp.float32)
        for head in range(heads):
            queries[pl.ds(piece * held * heads + head, held, stride=heads), :] = block[
                :, head * LANES : (head + 1) * LANES
            ]
    together = 2 if kv_heads % 2 == 0 else 1
    each = slots // key_scale_ref.shape[0]
    rows = together * group
    lane = lane_index((heads, LANES))
    token = lane_index((heads, page_tokens))
    upper = lax.broadcasted_iota(jnp.int32, (rows, LANES), 0) < group
    zero = jnp.zeros((rows, LANES), jnp.bfloat16)
    logs = jnp.zeros((heads, LANES), jnp.float32)

    lives = [
        jnp.broadcast_to(located_ref[1:2, slot : slot + 1], (heads, page_tokens))
        for slot in range(slots)
    ]

    def joined(ref, slot, kv):
        if together == 1:
            return ref[slot, kv]
        return jnp.concatenate([ref[slot, kv], ref[slot, kv + 1]], axis=1)

    def products(batch):
        dotted = []
        for index in range(each):
            slot = batch * each + index
            start = pl.multiple_of(located_ref[0, slot] * heads, 8)
            query = queries[pl.ds(start, heads), :].astype(jnp.bfloat16)
            for kv in range(0, kv_heads, together):
                own = query[kv * group : kv * group + rows]
                if together == 2:
                    own = jnp.concatenate(
                        [jnp.where(upper, own, zero), jnp.where(upper, zero, own)], axis=1
                    )
                dotted.append(
                    lax.dot_general(
                        own,
                        joined(key_ref, slot, kv),
                        (((1,), (1,)), ((), ())),
                        preferred_element_type=jnp.float32,
                    )
                )
        return jnp.concatenate(dotted, axis=0)

    def softmax(batch, dotted):
        scores = []
        for page in range(pages):
            part = dotted[:, page * page_tokens : (page + 1) * page_tokens]
            part = part * key_scale_ref[batch, page]
            masked = []
            for index in range(each):
                own = part[index * heads : (index + 1) * heads]
                live = lives[batch * each + index]
                masked.append(jnp.where(token + page * page_tokens < live, own, LOW))
            scores.append(jnp.concatenate(masked, axis=0) if each > 1 else masked[0])
        peak = jnp.max(functools.reduce(jnp.maximum, scores), axis=1, keepdims=True)
        total, weights = None, []
        for page in range(pages):
            expon = jnp.exp(scores[page] - peak)
            total = expon if total is None else total + expon
            weights.append((expon * value_scale_ref[batch, page]).astype(jnp.bfloat16))
        total = jnp.sum(total, axis=1, keepdims=True)
        return jnp.concatenate(weights, axis=1), 1.0 / total, peak + jnp.log(total)

    def sums(batch, weights, scale):
        for index in range(each):
            slot = batch * each + index
            for kv in range(0, kv_heads, together):
                first = index * heads + kv * group
                partial = jnp.dot(
                    weights[first : first + rows],
                    joined(value_ref, slot, kv),
                    preferred_element_type=jnp.float32,
                )
                if together == 2:
                    partial = jnp.concatenate(
                        [partial[:group, :LANES], partial[group:, LANES:]], axis=0
                    )
                at = slot * heads + kv * group
                outs[at : at + rows, :] = partial * scale[first : first + rows]

    batches = key_scale_ref.shape[0]
    ready = products(0)
    for batch in range(batches):
        following = products(batch + 1) if batch + 1 < batches else None
        weights, scale, log = softmax(batch, ready)
        sums(batch, weights, scale)
        ready = following
        for index in range(each):
            slot = batch * each + index
            logs = jnp.where(lane == slot, log[index * heads : (index + 1) * heads], logs)

    out_ref[: slots * heads, :] = outs[...].astype(jnp.bfloat16)
    store_stats(out_ref, slots * heads, logs, slots, heads)


def merge_slots_kernel(groups, slots, rows, heads, located_ref, *refs):
    out_ref, sums = refs[groups:]
    lane = lane_index((heads, LANES))
    owner = jnp.broadcast_to(located_ref[2:3, :], (heads, LANES))
    logs = jnp.full((heads, LANES), LOW, jnp.float32)
    for index in range(groups):
        own = load_stats(refs[index], slots * heads, slots, heads)
        own = pltpu.roll(own, index * slots, 1) if index else own
        inside = (lane >= index * slots) & (lane < (index + 1) * slots)
        logs = jnp.where(inside, own, logs)
    tops = jnp.zeros((heads, LANES), jnp.float32)
    row_top = []
    for row in range(rows):
        top = jnp.max(jnp.where(owner == row, logs, LOW), axis=1, keepdims=True)
        tops = jnp.where(owner == row, top, tops)
        row_top.append(top)
    factor = jnp.exp(logs - tops)
    totals = jnp.ones((heads, LANES), jnp.float32)
    row_logs = jnp.full((heads, LANES), LOW, jnp.float32)
    for row in range(rows):
        total = jnp.sum(jnp.where(owner == row, factor, 0.0), axis=1, keepdims=True)
        totals = jnp.where(owner == row, total, totals)
        held = total > 0.0
        value = jnp.where(held, row_top[row] + jnp.log(jnp.where(held, total, 1.0)), LOW)
        row_logs = jnp.where(lane == row, value, row_logs)
    weight = factor / totals
    sums[...] = jnp.zeros_like(sums)
    for index in range(groups):
        for slot in range(slots):
            at = index * slots + slot
            start = pl.multiple_of(located_ref[2, at] * heads, 8)
            block = pl.ds(start, heads)
            sums[block, :] += weight[:, at : at + 1] * load_entry(refs[index], slot, heads)
    out_ref[: rows * heads, :] = sums[...].astype(jnp.bfloat16)
    store_stats(out_ref, rows * heads, row_logs, rows, heads)


def merge_rows(refs, rows, heads, sums):
    logs = [load_stats(ref, rows * heads, rows, heads) for ref in refs]
    top = functools.reduce(jnp.maximum, logs)
    factors = [jnp.exp(log - top) for log in logs]
    total = functools.reduce(jnp.add, factors)
    weights = [factor / total for factor in factors]
    for row in range(rows):
        parts = [
            weight[:, row : row + 1] * load_entry(ref, row, heads)
            for weight, ref in zip(weights, refs)
        ]
        sums[row * heads : (row + 1) * heads, :] = functools.reduce(jnp.add, parts)
    return top + jnp.log(total)


def merge_rows_kernel(groups, rows, heads, *refs):
    out_ref, sums = refs[groups:]
    logs = merge_rows(refs[:groups], rows, heads, sums)
    out_ref[: rows * heads, :] = sums[...].astype(jnp.bfloat16)
    store_stats(out_ref, rows * heads, logs, rows, heads)


def project_kernel(groups, rows, heads, halves, *refs):
    weight_ref, *out_refs, sums = refs[groups:]
    merge_rows(refs[:groups], rows, heads, sums)
    attention = jnp.concatenate(
        [sums[pl.ds(head, rows, stride=heads), :].astype(jnp.bfloat16) for head in range(heads)],
        axis=1,
    )
    mixed = jnp.dot(attention, weight_ref[...], preferred_element_type=jnp.float32)
    if halves:
        first = lax.axis_index("head") == 0
        lower, upper = mixed[: rows // 2], mixed[rows // 2 :]
        out_refs[0][...] = jnp.where(first, lower, upper)
        out_refs[1][...] = jnp.where(first, upper, lower)
    else:
        out_refs[0][...] = mixed


def per_device(
    query,
    key_codes,
    value_codes,
    key_scale,
    value_scale,
    out_weight,
    range_counts,
    last_fill,
    slot_table,
    *,
    devices,
    head_devices,
):
    slots, kv_heads, tokens, head_dim = key_codes.shape
    pages = key_scale.shape[2]
    rows = range_counts.shape[0]
    all_slots = slot_table.shape[0]
    heads = query.shape[1] // head_dim
    group = heads // kv_heads
    own_rows = query.shape[0]
    columns = out_weight.shape[1]
    spread = spread_rounds(devices)
    rounds = [exchange_masks(bits) for bits in merge_rounds(devices)]

    near = [0] + rounds[0]
    tables = jnp.concatenate([range_counts, last_fill, slot_table])
    located = pl.pallas_call(
        functools.partial(
            locate_kernel, sum(spread, []), near, slots, rows, all_slots, own_rows, tokens
        ),
        out_shape=jax.ShapeDtypeStruct((8, LANES), jnp.int32),
        in_specs=[SMEM],
        out_specs=VMEM,
        scratch_shapes=[
            pltpu.SMEM((all_slots,), jnp.int32),
            pltpu.SMEM((rows,), jnp.int32),
        ],
        cost_estimate=pl.CostEstimate(
            flops=LOCATE_FLOPS, bytes_accessed=4 * all_slots, transcendentals=0
        ),
        compiler_params=pltpu.CompilerParams(vmem_limit_bytes=MIB),
        name="locate",
    )(tables)

    batches = slots // 2 if slots % 2 == 0 else slots
    scales = pl.pallas_call(
        functools.partial(columns_kernel, group, head_dim**-0.5),
        out_shape=[
            jax.ShapeDtypeStruct(
                (batches, pages, slots // batches * heads, LANES), jnp.float32
            )
        ]
        * 2,
        in_specs=[VMEM] * 2,
        out_specs=[VMEM] * 2,
        compiler_params=pltpu.CompilerParams(vmem_limit_bytes=2 * MIB),
        name="columns",
    )(key_scale, value_scale)

    held = [query]
    for turn, bits in enumerate(spread):
        block = jnp.concatenate(held, axis=0) if len(held) > 1 else held[0]
        if turn == 1:
            block, located = lax.optimization_barrier((block, located))
        elif turn > 1:
            block = lax.optimization_barrier(block)
        held = [block] + [partner(block, mask, devices) for mask in exchange_masks(bits)]

    payload = (slots + stat_blocks(slots)) * heads
    held = [
        pl.pallas_call(
            functools.partial(
                attend_kernel, len(held), slots, kv_heads, group, tokens, pages
            ),
            out_shape=jax.ShapeDtypeStruct((payload, LANES), jnp.bfloat16),
            in_specs=[VMEM] * (len(held) + 5),
            out_specs=VMEM,
            scratch_shapes=[
                pltpu.VMEM((rows * heads, LANES), jnp.float32),
                pltpu.VMEM((slots * heads, LANES), jnp.float32),
            ],
            compiler_params=pltpu.CompilerParams(vmem_limit_bytes=8 * MIB),
            cost_estimate=pl.CostEstimate(
                flops=ATTEND_FLOPS,
                bytes_accessed=4 * slots * kv_heads * tokens * head_dim,
                transcendentals=slots * heads * tokens,
            ),
            name="attend",
        )(
            located,
            *scales,
            *held,
            key_codes,
            value_codes,
        )
    ]

    payload = (rows + stat_blocks(rows)) * heads
    sums = pltpu.VMEM((rows * heads, LANES), jnp.float32)
    for turn, masks in enumerate(rounds):
        held = held + [partner(held[0], mask, devices) for mask in masks]
        groups = len(held)
        params = pltpu.CompilerParams(vmem_limit_bytes=8 * MIB)
        if turn == 0:
            held = [
                pl.pallas_call(
                    functools.partial(merge_slots_kernel, groups, slots, rows, heads),
                    out_shape=jax.ShapeDtypeStruct((payload, LANES), jnp.bfloat16),
                    in_specs=[VMEM] * (groups + 1),
                    out_specs=VMEM,
                    scratch_shapes=[sums],
                    compiler_params=params,
                    cost_estimate=pl.CostEstimate(
                        flops=MERGE_FLOPS, bytes_accessed=2 * payload * LANES, transcendentals=0
                    ),
                    name="merge_slots",
                )(located, *held)
            ]
        elif turn < len(rounds) - 1:
            held = [
                pl.pallas_call(
                    functools.partial(merge_rows_kernel, groups, rows, heads),
                    out_shape=jax.ShapeDtypeStruct((payload, LANES), jnp.bfloat16),
                    in_specs=[VMEM] * groups,
                    out_specs=VMEM,
                    scratch_shapes=[sums],
                    compiler_params=params,
                    name="merge_rows",
                )(*held)
            ]
    halves = head_devices == 2
    mixed_shape = jax.ShapeDtypeStruct((rows // (1 + halves), columns), jnp.float32)
    mixed, *give = pl.pallas_call(
        functools.partial(project_kernel, len(held), rows, heads, halves),
        out_shape=[mixed_shape] * (1 + halves),
        in_specs=[VMEM] * (len(held) + 1),
        out_specs=[VMEM] * (1 + halves),
        scratch_shapes=[sums],
        compiler_params=pltpu.CompilerParams(vmem_limit_bytes=8 * MIB),
        name="project",
    )(*held, out_weight)
    if halves:
        mixed = mixed + lax.ppermute(give[0], "head", [(0, 1), (1, 0)])
    else:
        mixed = lax.psum_scatter(mixed, "head", scatter_dimension=0, tiled=True)
    return mixed.astype(jnp.bfloat16)


def solution(mesh):
    return jax.shard_map(
        functools.partial(
            per_device, devices=mesh.shape["page"], head_devices=mesh.shape["head"]
        ),
        mesh=mesh,
        in_specs=(
            P("page", "head"),
            P("page", "head", None, None),
            P("page", "head", None, None),
            P("page", "head", None),
            P("page", "head", None),
            P("head", "page"),
            P(),
            P(),
            P(),
        ),
        out_specs=P("head", "page"),
        check_vma=False,
    )
```

```python
import functools

import jax
import jax.numpy as jnp
from jax import lax
from jax.experimental import pallas as pl
from jax.experimental.pallas import tpu as pltpu
from jax.sharding import PartitionSpec as P

LANES = 128
LOW = -1e30
LOCATE_FLOPS = 20_000_000_000
ATTEND_FLOPS = 5_000_000_000
MERGE_FLOPS = 20_000_000_000
MIB = 1 << 20
VMEM = pl.BlockSpec(memory_space=pltpu.VMEM)
SMEM = pl.BlockSpec(memory_space=pltpu.SMEM)


def exchange_masks(bits):
    masks = [0]
    for bit in bits:
        masks += [mask + bit for mask in masks]
    return masks[1:]


def spread_rounds(devices):
    bits = [1 << k for k in range(devices.bit_length() - 1)]
    return [bits[:2]] + [bits[k : k + 2] for k in range(2, len(bits), 2)]


def merge_rounds(devices):
    bits = [1 << k for k in range(devices.bit_length() - 1)]
    pairs = [[bits[-1 - k], bits[k]] for k in range(len(bits) // 2)]
    pairs[0] = pairs[0][::-1]
    return pairs + ([[bits[len(bits) // 2]]] if len(bits) % 2 else [])


def partner(value, mask, devices):
    return lax.ppermute(value, "page", [(i, i ^ mask) for i in range(devices)])


def stat_place(piece, entries):
    each = LANES // entries
    return piece // each, (piece % each) * entries


def stat_blocks(entries):
    return stat_place(2, entries)[0] + 1


def stat_fold(entries, heads):
    width = LANES
    if stat_blocks(entries) == 1 and heads % 32 == 0:
        while width // 2 >= 3 * entries and width > LANES // 4:
            width //= 2
    return LANES // width, width


def stat_rows(entries, heads):
    rows = stat_blocks(entries) * heads // stat_fold(entries, heads)[0]
    return (rows + 15) // 16 * 16


def lane_index(shape):
    return lax.broadcasted_iota(jnp.int32, shape, 1)


def store_stats(out_ref, base, logs, entries, heads):
    high = logs.astype(jnp.bfloat16).astype(jnp.float32)
    middle = (logs - high).astype(jnp.bfloat16).astype(jnp.float32)
    low = logs - high - middle
    fold, width = stat_fold(entries, heads)
    size = heads // fold
    lane = lane_index((size, LANES))
    blocks = [jnp.zeros((size, LANES), jnp.float32) for _ in range(stat_blocks(entries))]
    for piece, value in enumerate((high, middle, low)):
        block, offset = stat_place(piece, entries)
        for k in range(fold):
            first = offset + k * width
            slab = value[k * size : (k + 1) * size]
            slab = pltpu.roll(slab, first, 1) if first else slab
            inside = (lane >= first) & (lane < first + entries)
            blocks[block] = jnp.where(inside, slab, blocks[block])
    rest = stat_rows(entries, heads) - size * len(blocks)
    if rest:
        blocks.append(jnp.zeros((rest, LANES), jnp.float32))
    table = jnp.concatenate(blocks, axis=0) if len(blocks) > 1 else blocks[0]
    out_ref[base : base + table.shape[0], :] = table.astype(jnp.bfloat16)


def load_stats(ref, base, entries, heads, shift=0):
    table = ref[base : base + stat_rows(entries, heads), :].astype(jnp.float32)
    fold, width = stat_fold(entries, heads)
    size = heads // fold
    slabs = []
    for k in range(fold):
        total = None
        for piece in range(3):
            block, offset = stat_place(piece, entries)
            value = table[block * size : (block + 1) * size]
            move = (shift - offset - k * width) % LANES
            value = pltpu.roll(value, move, 1) if move else value
            total = value if total is None else total + value
        slabs.append(total)
    return jnp.concatenate(slabs, axis=0) if fold > 1 else slabs[0]


def load_entry(ref, index, heads):
    if heads % 16 == 0:
        return ref[index * heads : (index + 1) * heads, :].astype(jnp.float32)
    base = index * heads // 16 * 16
    block = ref[base : base + 16, :].astype(jnp.float32)
    return block[index * heads - base : (index + 1) * heads - base]


def locate_kernel(
    bits, near, slots, rows, all_slots, own_rows, tokens,
    table_ref, out_ref, position_of, first_of,
):
    me = lax.axis_index("page")
    fills, entries = rows, 2 * rows
    lane = lane_index((1, LANES))
    places = jnp.zeros((1, LANES), jnp.int32)
    lives = jnp.zeros((1, LANES), jnp.int32)
    owners = jnp.full((1, LANES), -1, jnp.int32)

    def note(position, carry):
        position_of[table_ref[entries + position]] = position
        return carry

    lax.fori_loop(0, all_slots, note, 0, unroll=16)
    ends, end = [], jnp.int32(0)
    for row in range(rows):
        first_of[row] = end
        end = end + table_ref[row]
        ends.append(end)
    for index, mask in enumerate(near):
        source = jnp.bitwise_xor(me, mask)
        for slot in range(slots):
            position = position_of[source * slots + slot]
            row = functools.reduce(
                jnp.add, [(position >= end).astype(jnp.int32) for end in ends[:-1]]
            )
            owners = jnp.where(lane == index * slots + slot, row, owners)
            if index == 0:
                away = jnp.bitwise_xor(row // own_rows, me)
                place, step_size = row % own_rows, own_rows
                for bit in bits:
                    place += away // bit % 2 * step_size
                    step_size *= 2
                places = jnp.where(lane == slot, place, places)
                before = position - first_of[row]
                live = (table_ref[row] - 1 - before) * tokens + table_ref[fills + row]
                lives = jnp.where(lane == slot, live, lives)
    out_ref[...] = jnp.concatenate(
        [places, lives, owners, jnp.zeros((5, LANES), jnp.int32)], axis=0
    )


def columns_kernel(group, factor, *refs):
    for scale_ref, out_ref, multiplier in zip(refs[:2], refs[2:], (factor, 1.0)):
        slots, kv_heads, pages = scale_ref.shape
        batches = out_ref.shape[0]
        each = slots // batches
        for batch in range(batches):
            parts = []
            for index in range(each):
                scale = scale_ref[batch * each + index] * multiplier
                for kv in range(kv_heads):
                    parts.append(jnp.broadcast_to(scale[kv : kv + 1], (group, pages)))
            table = jnp.concatenate(parts, axis=0)
            for page in range(pages):
                out_ref[batch, page] = jnp.broadcast_to(
                    table[:, page : page + 1], (table.shape[0], LANES)
                )


def attend_kernel(
    pieces, slots, kv_heads, group, tokens, pages,
    located_ref, key_scale_ref, value_scale_ref, *refs,
):
    query_refs = refs[:pieces]
    key_ref, value_ref, out_ref, queries, outs = refs[pieces:]
    heads = kv_heads * group
    page_tokens = tokens // pages
    held = query_refs[0].shape[0]
    for piece, query_ref in enumerate(query_refs):
        block = query_ref[...].astype(jnp.float32)
        for head in range(heads):
            queries[pl.ds(piece * held * heads + head, held, stride=heads), :] = block[
                :, head * LANES : (head + 1) * LANES
            ]
    together = 2 if kv_heads % 2 == 0 else 1
    each = slots // key_scale_ref.shape[0]
    rows = together * group
    lane = lane_index((heads, LANES))
    token = lane_index((heads, page_tokens))
    upper = lax.broadcasted_iota(jnp.int32, (rows, LANES), 0) < group
    zero = jnp.zeros((rows, LANES), jnp.bfloat16)
    logs = jnp.zeros((heads, LANES), jnp.float32)

    lives = [
        jnp.broadcast_to(located_ref[1:2, slot : slot + 1], (heads, page_tokens))
        for slot in range(slots)
    ]

    def joined(ref, slot, kv):
        if together == 1:
            return ref[slot, kv]
        return jnp.concatenate([ref[slot, kv], ref[slot, kv + 1]], axis=1)

    def products(batch):
        dotted = []
        for index in range(each):
            slot = batch * each + index
            start = pl.multiple_of(located_ref[0, slot] * heads, 8)
            query = queries[pl.ds(start, heads), :].astype(jnp.bfloat16)
            for kv in range(0, kv_heads, together):
                own = query[kv * group : kv * group + rows]
                if together == 2:
                    own = jnp.concatenate(
                        [jnp.where(upper, own, zero), jnp.where(upper, zero, own)], axis=1
                    )
                dotted.append(
                    lax.dot_general(
                        own,
                        joined(key_ref, slot, kv),
                        (((1,), (1,)), ((), ())),
                        preferred_element_type=jnp.float32,
                    )
                )
        return jnp.concatenate(dotted, axis=0)

    def softmax(batch, dotted):
        scores = []
        for page in range(pages):
            part = dotted[:, page * page_tokens : (page + 1) * page_tokens]
            part = part * key_scale_ref[batch, page]
            masked = []
            for index in range(each):
                own = part[index * heads : (index + 1) * heads]
                live = lives[batch * each + index]
                masked.append(jnp.where(token + page * page_tokens < live, own, LOW))
            scores.append(jnp.concatenate(masked, axis=0) if each > 1 else masked[0])
        peak = jnp.max(functools.reduce(jnp.maximum, scores), axis=1, keepdims=True)
        total, weights = None, []
        for page in range(pages):
            expon = jnp.exp(scores[page] - peak)
            total = expon if total is None else total + expon
            weights.append((expon * value_scale_ref[batch, page]).astype(jnp.bfloat16))
        total = jnp.sum(total, axis=1, keepdims=True)
        return jnp.concatenate(weights, axis=1), 1.0 / total, peak + jnp.log(total)

    def sums(batch, weights, scale):
        for index in range(each):
            slot = batch * each + index
            for kv in range(0, kv_heads, together):
                first = index * heads + kv * group
                partial = jnp.dot(
                    weights[first : first + rows],
                    joined(value_ref, slot, kv),
                    preferred_element_type=jnp.float32,
                )
                if together == 2:
                    partial = jnp.concatenate(
                        [partial[:group, :LANES], partial[group:, LANES:]], axis=0
                    )
                at = slot * heads + kv * group
                outs[at : at + rows, :] = partial * scale[first : first + rows]

    batches = key_scale_ref.shape[0]
    ready = products(0)
    for batch in range(batches):
        following = products(batch + 1) if batch + 1 < batches else None
        weights, scale, log = softmax(batch, ready)
        sums(batch, weights, scale)
        ready = following
        for index in range(each):
            slot = batch * each + index
            logs = jnp.where(lane == slot, log[index * heads : (index + 1) * heads], logs)

    out_ref[: slots * heads, :] = outs[...].astype(jnp.bfloat16)
    store_stats(out_ref, slots * heads, logs, slots, heads)


def merge_slots_kernel(groups, slots, rows, heads, located_ref, *refs):
    out_ref, sums = refs[groups:]
    lane = lane_index((heads, LANES))
    owner = jnp.broadcast_to(located_ref[2:3, :], (heads, LANES))
    logs = jnp.full((heads, LANES), LOW, jnp.float32)
    for index in range(groups):
        own = load_stats(refs[index], slots * heads, slots, heads, index * slots)
        inside = (lane >= index * slots) & (lane < (index + 1) * slots)
        logs = jnp.where(inside, own, logs)
    tops = jnp.zeros((heads, LANES), jnp.float32)
    row_top = []
    for row in range(rows):
        top = jnp.max(jnp.where(owner == row, logs, LOW), axis=1, keepdims=True)
        tops = jnp.where(owner == row, top, tops)
        row_top.append(top)
    factor = jnp.exp(logs - tops)
    totals = jnp.ones((heads, LANES), jnp.float32)
    row_logs = jnp.full((heads, LANES), LOW, jnp.float32)
    for row in range(rows):
        total = jnp.sum(jnp.where(owner == row, factor, 0.0), axis=1, keepdims=True)
        totals = jnp.where(owner == row, total, totals)
        held = total > 0.0
        value = jnp.where(held, row_top[row] + jnp.log(jnp.where(held, total, 1.0)), LOW)
        row_logs = jnp.where(lane == row, value, row_logs)
    weight = factor / totals
    sums[...] = jnp.zeros_like(sums)
    for index in range(groups):
        for slot in range(slots):
            at = index * slots + slot
            start = pl.multiple_of(located_ref[2, at] * heads, 8)
            block = pl.ds(start, heads)
            sums[block, :] += weight[:, at : at + 1] * load_entry(refs[index], slot, heads)
    out_ref[: rows * heads, :] = sums[...].astype(jnp.bfloat16)
    store_stats(out_ref, rows * heads, row_logs, rows, heads)


def merge_rows(refs, rows, heads, sums):
    logs = [load_stats(ref, rows * heads, rows, heads) for ref in refs]
    top = functools.reduce(jnp.maximum, logs)
    factors = [jnp.exp(log - top) for log in logs]
    total = functools.reduce(jnp.add, factors)
    weights = [factor / total for factor in factors]
    for row in range(rows):
        parts = [
            weight[:, row : row + 1] * load_entry(ref, row, heads)
            for weight, ref in zip(weights, refs)
        ]
        sums[row * heads : (row + 1) * heads, :] = functools.reduce(jnp.add, parts)
    return top + jnp.log(total)


def merge_rows_kernel(groups, rows, heads, *refs):
    out_ref, sums = refs[groups:]
    logs = merge_rows(refs[:groups], rows, heads, sums)
    out_ref[: rows * heads, :] = sums[...].astype(jnp.bfloat16)
    store_stats(out_ref, rows * heads, logs, rows, heads)


def project_kernel(groups, rows, heads, halves, *refs):
    weight_ref, *out_refs, sums = refs[groups:]
    merge_rows(refs[:groups], rows, heads, sums)
    attention = jnp.concatenate(
        [sums[pl.ds(head, rows, stride=heads), :].astype(jnp.bfloat16) for head in range(heads)],
        axis=1,
    )
    mixed = jnp.dot(attention, weight_ref[...], preferred_element_type=jnp.float32)
    if halves:
        first = lax.axis_index("head") == 0
        lower, upper = mixed[: rows // 2], mixed[rows // 2 :]
        out_refs[0][...] = jnp.where(first, lower, upper)
        out_refs[1][...] = jnp.where(first, upper, lower)
    else:
        out_refs[0][...] = mixed


def per_device(
    query,
    key_codes,
    value_codes,
    key_scale,
    value_scale,
    out_weight,
    range_counts,
    last_fill,
    slot_table,
    *,
    devices,
    head_devices,
):
    slots, kv_heads, tokens, head_dim = key_codes.shape
    pages = key_scale.shape[2]
    rows = range_counts.shape[0]
    all_slots = slot_table.shape[0]
    heads = query.shape[1] // head_dim
    group = heads // kv_heads
    own_rows = query.shape[0]
    columns = out_weight.shape[1]
    spread = spread_rounds(devices)
    rounds = [exchange_masks(bits) for bits in merge_rounds(devices)]

    near = [0] + rounds[0]
    tables = jnp.concatenate([range_counts, last_fill, slot_table])
    located = pl.pallas_call(
        functools.partial(
            locate_kernel, sum(spread, []), near, slots, rows, all_slots, own_rows, tokens
        ),
        out_shape=jax.ShapeDtypeStruct((8, LANES), jnp.int32),
        in_specs=[SMEM],
        out_specs=VMEM,
        scratch_shapes=[
            pltpu.SMEM((all_slots,), jnp.int32),
            pltpu.SMEM((rows,), jnp.int32),
        ],
        cost_estimate=pl.CostEstimate(
            flops=LOCATE_FLOPS, bytes_accessed=4 * all_slots, transcendentals=0
        ),
        compiler_params=pltpu.CompilerParams(vmem_limit_bytes=MIB),
        name="locate",
    )(tables)

    batches = slots // 2 if slots % 2 == 0 else slots
    scales = pl.pallas_call(
        functools.partial(columns_kernel, group, head_dim**-0.5),
        out_shape=[
            jax.ShapeDtypeStruct(
                (batches, pages, slots // batches * heads, LANES), jnp.float32
            )
        ]
        * 2,
        in_specs=[VMEM] * 2,
        out_specs=[VMEM] * 2,
        compiler_params=pltpu.CompilerParams(vmem_limit_bytes=2 * MIB),
        name="columns",
    )(key_scale, value_scale)

    held = [query]
    for turn, bits in enumerate(spread):
        block = jnp.concatenate(held, axis=0) if len(held) > 1 else held[0]
        if turn == 1:
            block, located = lax.optimization_barrier((block, located))
        elif turn > 1:
            block = lax.optimization_barrier(block)
        held = [block] + [partner(block, mask, devices) for mask in exchange_masks(bits)]

    payload = slots * heads + stat_rows(slots, heads)
    held = [
        pl.pallas_call(
            functools.partial(
                attend_kernel, len(held), slots, kv_heads, group, tokens, pages
            ),
            out_shape=jax.ShapeDtypeStruct((payload, LANES), jnp.bfloat16),
            in_specs=[VMEM] * (len(held) + 5),
            out_specs=VMEM,
            scratch_shapes=[
                pltpu.VMEM((rows * heads, LANES), jnp.float32),
                pltpu.VMEM((slots * heads, LANES), jnp.float32),
            ],
            compiler_params=pltpu.CompilerParams(vmem_limit_bytes=8 * MIB),
            cost_estimate=pl.CostEstimate(
                flops=ATTEND_FLOPS,
                bytes_accessed=4 * slots * kv_heads * tokens * head_dim,
                transcendentals=slots * heads * tokens,
            ),
            name="attend",
        )(
            located,
            *scales,
            *held,
            key_codes,
            value_codes,
        )
    ]

    payload = rows * heads + stat_rows(rows, heads)
    sums = pltpu.VMEM((rows * heads, LANES), jnp.float32)
    for turn, masks in enumerate(rounds):
        held = held + [partner(held[0], mask, devices) for mask in masks]
        groups = len(held)
        params = pltpu.CompilerParams(vmem_limit_bytes=8 * MIB)
        if turn == 0:
            held = [
                pl.pallas_call(
                    functools.partial(merge_slots_kernel, groups, slots, rows, heads),
                    out_shape=jax.ShapeDtypeStruct((payload, LANES), jnp.bfloat16),
                    in_specs=[VMEM] * (groups + 1),
                    out_specs=VMEM,
                    scratch_shapes=[sums],
                    compiler_params=params,
                    cost_estimate=pl.CostEstimate(
                        flops=MERGE_FLOPS, bytes_accessed=2 * payload * LANES, transcendentals=0
                    ),
                    name="merge_slots",
                )(located, *held)
            ]
        elif turn < len(rounds) - 1:
            held = [
                pl.pallas_call(
                    functools.partial(merge_rows_kernel, groups, rows, heads),
                    out_shape=jax.ShapeDtypeStruct((payload, LANES), jnp.bfloat16),
                    in_specs=[VMEM] * groups,
                    out_specs=VMEM,
                    scratch_shapes=[sums],
                    compiler_params=params,
                    name="merge_rows",
                )(*held)
            ]
    halves = head_devices == 2
    mixed_shape = jax.ShapeDtypeStruct((rows // (1 + halves), columns), jnp.float32)
    mixed, *give = pl.pallas_call(
        functools.partial(project_kernel, len(held), rows, heads, halves),
        out_shape=[mixed_shape] * (1 + halves),
        in_specs=[VMEM] * (len(held) + 1),
        out_specs=[VMEM] * (1 + halves),
        scratch_shapes=[sums],
        compiler_params=pltpu.CompilerParams(vmem_limit_bytes=8 * MIB),
        name="project",
    )(*held, out_weight)
    if halves:
        mixed = mixed + lax.ppermute(give[0], "head", [(0, 1), (1, 0)])
    else:
        mixed = lax.psum_scatter(mixed, "head", scatter_dimension=0, tiled=True)
    return mixed.astype(jnp.bfloat16)


def solution(mesh):
    return jax.shard_map(
        functools.partial(
            per_device, devices=mesh.shape["page"], head_devices=mesh.shape["head"]
        ),
        mesh=mesh,
        in_specs=(
            P("page", "head"),
            P("page", "head", None, None),
            P("page", "head", None, None),
            P("page", "head", None),
            P("page", "head", None),
            P("head", "page"),
            P(),
            P(),
            P(),
        ),
        out_specs=P("head", "page"),
        check_vma=False,
    )
```
